256 devices in a mesh: seq: 64 (over y_lo, x, z), batch: 4 (over y_hi, core).
Axes of the slice: x: 4, y: 4 (y_hi: 2, y_lo: 2; y = y_hi * 2 + y_lo), z: 8, core: 2. Of those that a mesh axis runs over, the one named last changes fastest.
Arguments:
- inputs: bfloat16 [4, 32768, 768], P('batch', 'seq'), may hold values from -6 to 6
- upstream: bfloat16 [4, 32768, 768], P('batch', 'seq'), may hold values from -6 to 6
- first_spread_weight: bfloat16 [3, 768, 384], P(None, ('seq', 'batch')), may hold values from -0.125 to 0.125
- first_pointwise_weight: bfloat16 [768, 384], P(('seq', 'batch')), may hold values from -0.3125 to 0.3125
- second_spread_weight: bfloat16 [3, 768, 384], P(None, ('seq', 'batch')), may hold values from -0.125 to 0.125
- second_pointwise_weight: bfloat16 [768, 384], P(('seq', 'batch')), may hold values from -0.3125 to 0.3125
Outputs:
- outputs: bfloat16 [4, 32768, 768], P('batch', 'seq')
- input_cotangent_array: bfloat16 [4, 32768, 768], P('batch', 'seq')
- wide_first_grad: bfloat16 [3, 768, 384], P(None, ('seq', 'batch'))
- narrow_first_grad: bfloat16 [768, 384], P(('seq', 'batch'))
- wide_second_grad: bfloat16 [3, 768, 384], P(None, ('seq', 'batch'))
- narrow_second_grad: bfloat16 [768, 384], P(('seq', 'batch'))
The draws below stay inside these ranges and needn't reach their ends.
All inputs are finite; a program needn't handle non-finite values.
Results may differ from the reference program's by a relative error of at most 0.02.
Values may be sent and summed in bfloat16 or wider, within the bound.
No kernel may reach another device: no remote copies, remote signals or barrier semaphores. Data moves between devices by JAX's collectives and lax.ppermute only.
A program may use at most 128 MiB of HBM per device.

```python
import jax
import jax.numpy as jnp
from jax import lax

D = 768
F = 384
LENGTH = 32768
SEQS = 4
FIRST_SPACING = 1024
SECOND_SPACING = 2048


def shard_levels(stream_key, extent, shards, least, high):
    factor_of = 1.0
    for axis_at, blocks in shards:
        draws = jax.random.uniform(jax.random.fold_in(jax.random.fold_in(stream_key, 6), axis_at), (blocks,), jnp.float32, least / len(shards), high / len(shards))
        factor_of = factor_of * jnp.repeat(jnp.exp(draws), extent[axis_at] // blocks).reshape((-1,) + (1,) * (len(extent) - 1 - axis_at))
    return factor_of


def noise(stream_key, extent, width, limit, shards=(), kind=jnp.bfloat16):
    factor_of = shard_levels(stream_key, extent, shards, -0.22, 0.18) if shards else 1.0
    values = jax.random.normal(stream_key, extent, jnp.float32) * width * factor_of
    return jnp.minimum(jnp.maximum(values, -limit), limit).astype(kind)


def setup_inputs(seed: int = 0) -> dict:
    arg_keys = jax.random.split(jax.random.key(seed), 7)
    return {
        "inputs": noise(arg_keys[0], (SEQS, LENGTH, D), 1.0, 6.0, ((0, 4), (1, 64))),
        "upstream": noise(arg_keys[1], (SEQS, LENGTH, D), 1.0, 6.0, ((0, 4), (1, 64))),
        "first_spread_weight": noise(arg_keys[2], (3, D, F), (3 * D) ** -0.5, 0.125, ((1, 256),)),
        "first_pointwise_weight": noise(arg_keys[3], (D, F), F ** -0.5, 0.3125, ((0, 256),)),
        "second_spread_weight": noise(arg_keys[4], (3, D, F), (3 * D) ** -0.5, 0.125, ((1, 256),)),
        "second_pointwise_weight": noise(arg_keys[5], (D, F), F ** -0.5, 0.3125, ((0, 256),)),
    }


def gelu_exact(v):
    return jax.nn.gelu(v, approximate=False)


def gelu_slope(v):
    cdf = 0.5 * (1.0 + lax.erf(v * 0.7071067811865476))
    return cdf + v * jnp.exp(-0.5 * v * v) * 0.3989422804014327


def lower_of(array, span):
    return jnp.pad(array, ((span, 0), (0, 0)))[: array.shape[0]]


def upper_of(array, span):
    return jnp.pad(array, ((0, span), (0, 0)))[span:]


def dot_plain(left, right):
    return jnp.dot(left, right, preferred_element_type=jnp.float32)


def dot_rows(left, right):
    return lax.dot_general(left, right, (((0,), (0,)), ((), ())), preferred_element_type=jnp.float32)


def dot_back(left, right):
    return lax.dot_general(left, right, (((1,), (1,)), ((), ())), preferred_element_type=jnp.float32)


def residual_block_apply(block_input, wide, narrow, span):
    act = gelu_exact(block_input.astype(jnp.float32)).astype(jnp.bfloat16)
    lower = lower_of(act, span)
    upper = upper_of(act, span)
    pre = dot_plain(lower, wide[0]) + dot_plain(act, wide[1]) + dot_plain(upper, wide[2])
    inner = gelu_exact(pre).astype(jnp.bfloat16)
    result = (block_input.astype(jnp.float32) + dot_back(inner, narrow)).astype(jnp.bfloat16)
    return result, (act, lower, upper, pre, inner)


def residual_block_reverse(block_input, saved, wide, narrow, span, incoming):
    act, lower, upper, pre, inner = saved
    narrow_grad = dot_rows(incoming, inner)
    dpre = (dot_plain(incoming, narrow) * gelu_slope(pre)).astype(jnp.bfloat16)
    wide_grad = jnp.stack([dot_rows(lower, dpre), dot_rows(act, dpre), dot_rows(upper, dpre)])
    dact = dot_back(upper_of(dpre, span), wide[0]) + dot_back(dpre, wide[1]) + dot_back(lower_of(dpre, span), wide[2])
    result = (incoming.astype(jnp.float32) + dact * gelu_slope(block_input.astype(jnp.float32))).astype(jnp.bfloat16)
    return result, wide_grad, narrow_grad


def reference(inputs, upstream, first_spread_weight, first_pointwise_weight, second_spread_weight, second_pointwise_weight):
    outs_list = []
    grads_list = []
    wide_one = jnp.zeros(first_spread_weight.shape, jnp.float32)
    narrow_one = jnp.zeros(first_pointwise_weight.shape, jnp.float32)
    wide_two = jnp.zeros(second_spread_weight.shape, jnp.float32)
    narrow_two = jnp.zeros(second_pointwise_weight.shape, jnp.float32)
    for block_index in range(SEQS):
        block_input = inputs[block_index]
        between_blocks, first_block_residuals = residual_block_apply(block_input, first_spread_weight, first_pointwise_weight, FIRST_SPACING)
        block_output, second_block_residuals = residual_block_apply(between_blocks, second_spread_weight, second_pointwise_weight, SECOND_SPACING)
        between_blocks_gradient, second_spread_gradient, second_pointwise_gradient = residual_block_reverse(between_blocks, second_block_residuals, second_spread_weight, second_pointwise_weight, SECOND_SPACING, upstream[block_index])
        input_cotangent_array, first_spread_gradient, first_pointwise_gradient = residual_block_reverse(block_input, first_block_residuals, first_spread_weight, first_pointwise_weight, FIRST_SPACING, between_blocks_gradient)
        wide_one = wide_one + first_spread_gradient
        narrow_one = narrow_one + first_pointwise_gradient
        wide_two = wide_two + second_spread_gradient
        narrow_two = narrow_two + second_pointwise_gradient
        outs_list.append(block_output)
        grads_list.append(input_cotangent_array)
    return (jnp.stack(outs_list), jnp.stack(grads_list), wide_one.astype(jnp.bfloat16), narrow_one.astype(jnp.bfloat16), wide_two.astype(jnp.bfloat16), narrow_two.astype(jnp.bfloat16))
```

```python
import jax
import jax.numpy as jnp
from jax import lax
from jax.sharding import Mesh, PartitionSpec as P

BF = jnp.bfloat16
F32 = jnp.float32
SEQ = ("yl", "x", "z")
RING_Y = ("yl", "yh")
COLS = 384
ROWS = 768


def gelu_parts(v):
    cdf = 0.5 * (1.0 + lax.erf(v * 0.7071067811865476))
    slope = cdf + v * jnp.exp(-0.5 * v * v) * 0.3989422804014327
    return v * cdf, slope


def dot_plain(left, right):
    return jnp.dot(left, right, preferred_element_type=F32)


def dot_rows(left, right):
    return lax.dot_general(left, right, (((0,), (0,)), ((), ())), preferred_element_type=F32)


def dot_back(left, right):
    return lax.dot_general(left, right, (((1,), (1,)), ((), ())), preferred_element_type=F32)


def shifted(array, by):
    count = lax.axis_size(SEQ)
    pairs = [(i, i + by) for i in range(count) if 0 <= i + by < count]
    return lax.ppermute(array, SEQ, pairs)


def hop(array, axis, by):
    count = lax.axis_size(axis)
    place = (lambda y: y % 2 * 2 + y // 2) if axis == RING_Y else (lambda i: i)
    pairs = [(place(i), place((i + by) % count)) for i in range(count)]
    return lax.ppermute(array, axis, pairs)


def collect(rows, axis):
    count = lax.axis_size(axis)
    return jnp.concatenate([rows] + [hop(rows, axis, k) for k in range(1, count)], axis=0)


def spread_sum(rows, axis):
    count = lax.axis_size(axis)
    size = rows.shape[0] // count
    total = rows[:size].astype(F32)
    for k in range(1, count):
        total = total + hop(rows[k * size : (k + 1) * size], axis, k).astype(F32)
    return total.astype(BF)


def slot_owner(sign):
    slot = lax.iota(jnp.int32, ROWS)
    row = slot % 3
    k = slot // 3
    kz, k = k % 8, k // 8
    kx, k = k % 4, k // 4
    ky, kc = k % 4, k // 4
    z = (lax.axis_index("z") + sign * kz + 8) % 8
    x = (lax.axis_index("x") + sign * kx + 4) % 4
    y = (lax.axis_index("yh") * 2 + lax.axis_index("yl") + sign * ky + 4) % 4
    c = (lax.axis_index("core") + sign * kc + 2) % 2
    yh, yl = y // 2, y % 2
    return ((((yl * 4 + x) * 8 + z) * 2 + yh) * 2 + c) * 3 + row


def body(inputs, upstream, wide_one, narrow_one, wide_two, narrow_two):
    x = inputs[0]
    g = upstream[0]

    def lanes(wide, narrow):
        return [wide[0], wide[1], wide[2], narrow]

    own = jnp.concatenate(lanes(wide_one, narrow_one) + lanes(wide_two, narrow_two), axis=1)
    rows_z = collect(own, "z")

    act1, slope_x = gelu_parts(x.astype(F32))
    act1 = act1.astype(BF)
    act1, rows_z = lax.optimization_barrier((act1, rows_z))
    lower1 = shifted(act1, 2)
    upper1 = shifted(act1, -2)

    rows_x = collect(rows_z, "x")
    channels = lax.iota(jnp.int32, ROWS)
    unmix = (slot_owner(-1)[None, :] == channels[:, None]).astype(BF)
    mix = (slot_owner(1)[None, :] == channels[:, None]).astype(BF)

    def kernels(rows):
        rows = collect(collect(rows, RING_Y), "core")
        return dot_plain(unmix, rows).astype(BF)

    k1 = kernels(rows_x[:, : 4 * COLS])
    k2 = kernels(rows_x[:, 4 * COLS :])

    def tap(k, i):
        return k[:, i * COLS : (i + 1) * COLS]

    def mixed(a):
        return dot_plain(a, mix).astype(BF)

    pre1 = (
        dot_plain(act1, tap(k1, 1))
        + dot_plain(lower1, tap(k1, 0))
        + dot_plain(upper1, tap(k1, 2))
    )
    inner1, slope1 = gelu_parts(pre1)
    inner1 = inner1.astype(BF)
    middle = (x.astype(F32) + dot_back(inner1, tap(k1, 3))).astype(BF)

    act2, slope_m = gelu_parts(middle.astype(F32))
    act2 = act2.astype(BF)
    to_later = shifted(dot_plain(act2, tap(k2, 0)).astype(BF), 4)
    to_earlier = shifted(dot_plain(act2, tap(k2, 2)).astype(BF), -4)
    pre2 = dot_plain(act2, tap(k2, 1)) + to_later.astype(F32) + to_earlier.astype(F32)
    inner2, slope2 = gelu_parts(pre2)
    inner2 = inner2.astype(BF)
    result = (middle.astype(F32) + dot_back(inner2, tap(k2, 3))).astype(BF)

    dpre2 = (dot_plain(g, tap(k2, 3)) * slope2).astype(BF)
    trio2 = jnp.concatenate([shifted(dpre2, -4), dpre2, shifted(dpre2, 4)], axis=1)
    dact2 = dot_back(trio2, k2[:, : 3 * COLS])
    middle_grad = (g.astype(F32) + dact2 * slope_m).astype(BF)
    grads2 = jnp.concatenate(
        [dot_rows(mixed(act2), trio2), dot_rows(mixed(g), inner2)], axis=1
    ).astype(BF)

    dpre1 = (dot_plain(middle_grad, tap(k1, 3)) * slope1).astype(BF)
    grads1 = jnp.concatenate(
        [
            dot_rows(mixed(lower1), dpre1),
            dot_rows(mixed(act1), dpre1),
            dot_rows(mixed(upper1), dpre1),
            dot_rows(mixed(middle_grad), inner1),
        ],
        axis=1,
    ).astype(BF)
    trio1 = jnp.concatenate([shifted(dpre1, -2), dpre1, shifted(dpre1, 2)], axis=1)
    dact1 = dot_back(trio1, k1[:, : 3 * COLS])
    cotangent = (middle_grad.astype(F32) + dact1 * slope_x).astype(BF)

    def partly(grads):
        return spread_sum(spread_sum(grads, "core"), RING_Y)

    both = jnp.concatenate([partly(grads1), partly(grads2)], axis=1)
    total = spread_sum(spread_sum(both, "x"), "z")

    def pick(first):
        return jnp.stack([total[:, (first + i) * COLS : (first + i + 1) * COLS] for i in range(3)])

    return (
        result[None],
        cotangent[None],
        pick(0),
        total[:, 3 * COLS : 4 * COLS],
        pick(4),
        total[:, 7 * COLS :],
    )


def solution(mesh):
    fine = Mesh(mesh.devices.reshape(2, 4, 8, 2, 2), ("yl", "x", "z", "yh", "core"))
    batch = ("yh", "core")
    specs = (
        P(batch, SEQ, None),
        P(batch, SEQ, None),
        P(None, SEQ + batch, None),
        P(SEQ + batch, None),
        P(None, SEQ + batch, None),
        P(SEQ + batch, None),
    )
    return jax.shard_map(body, mesh=fine, in_specs=specs, out_specs=specs, check_vma=False)
```

```python
import jax
import jax.numpy as jnp
from jax import lax
from jax.experimental import pallas as pl
from jax.experimental.pallas import tpu as pltpu
from jax.sharding import Mesh, PartitionSpec as P

BF = jnp.bfloat16
F32 = jnp.float32
LINE = ("yl", "x")
RING_Y = ("yl", "yh")
RING_Z = ("zq", "zp")
COLS = 384
ROWS = 768
QUARTER = 128


def gelu_parts(v):
    cdf = 0.5 * (1.0 + lax.erf(v * 0.7071067811865476))
    slope = cdf + v * jnp.exp(-0.5 * v * v) * 0.3989422804014327
    return v * cdf, slope


def dot_plain(left, right):
    return jnp.dot(left, right, preferred_element_type=F32)


def dot_rows(left, right):
    return lax.dot_general(left, right, (((0,), (0,)), ((), ())), preferred_element_type=F32)


def dot_back(left, right):
    return lax.dot_general(left, right, (((1,), (1,)), ((), ())), preferred_element_type=F32)


def along(array, by):
    count = lax.axis_size(LINE)
    pairs = [(i, i + by) for i in range(count) if 0 <= i + by < count]
    return lax.ppermute(array, LINE, pairs)


def hop(array, axis, by):
    count = lax.axis_size(axis)
    place = (lambda y: y % 2 * 2 + y // 2) if axis == RING_Y else (lambda i: i)
    pairs = [(place(i), place((i + by) % count)) for i in range(count)]
    return lax.ppermute(array, axis, pairs)


def exchange(array):
    me = lax.axis_index("zq")
    result = array
    for k in range(1, 4):
        there, back = (me + k) & 3, (me + 4 - k) & 3
        sent = lax.dynamic_slice_in_dim(array, there * QUARTER, QUARTER, 0)
        got = hop(sent, "zq", k)
        result = lax.dynamic_update_slice_in_dim(result, got, back * QUARTER, 0)
    return result


def collect(rows, axis):
    count = lax.axis_size(axis)
    return jnp.concatenate([rows] + [hop(rows, axis, k) for k in range(1, count)], axis=0)


def spread_sum(rows, axis):
    count = lax.axis_size(axis)
    size = rows.shape[0] // count
    got = [hop(rows[k * size : (k + 1) * size], axis, k) for k in range(1, count)]
    total = rows[:size].astype(F32)
    for piece in got:
        total = total + piece.astype(F32)
    return total.astype(BF)


def slot_owner(sign, x_first):
    slot = lax.iota(jnp.int32, ROWS)
    k = lax.div(slot, jnp.int32(3))
    row = slot - 3 * k
    z, k = k & 7, k >> 3
    kx, ky = ((k >> 2) & 3, k & 3) if x_first else (k & 3, (k >> 2) & 3)
    kc = k >> 4
    x = (lax.axis_index("x") + sign * kx + 4) & 3
    y = (lax.axis_index("yh") * 2 + lax.axis_index("yl") + sign * ky + 4) & 3
    c = (lax.axis_index("core") + sign * kc + 2) & 1
    yh, yl = y >> 1, y & 1
    return ((((yl * 4 + x) * 8 + z) * 2 + yh) * 2 + c) * 3 + row


def pack_kernel(wide_one, narrow_one, wide_two, narrow_two, out):
    for at, (wide, narrow) in enumerate(((wide_one, narrow_one), (wide_two, narrow_two))):
        for tap in range(3):
            out[:, (4 * at + tap) * COLS : (4 * at + tap + 1) * COLS] = wide[tap]
        out[:, (4 * at + 3) * COLS : (4 * at + 4) * COLS] = narrow[...]


def unpack_kernel(parts, wide_one, narrow_one, wide_two, narrow_two):
    total = parts[0].astype(F32)
    for k in range(1, 8):
        total = total + parts[k].astype(F32)
    total = total.astype(BF)
    for at, (wide, narrow) in enumerate(((wide_one, narrow_one), (wide_two, narrow_two))):
        for tap in range(3):
            wide[tap] = total[:, (4 * at + tap) * COLS : (4 * at + tap + 1) * COLS]
        narrow[...] = total[:, (4 * at + 3) * COLS : (4 * at + 4) * COLS]


def body(inputs, upstream, wide_one, narrow_one, wide_two, narrow_two):
    own = pl.pallas_call(
        pack_kernel, out_shape=jax.ShapeDtypeStruct((3, 8 * COLS), BF), name="pack_rows"
    )(wide_one, narrow_one, wide_two, narrow_two)
    rows_z = lax.all_to_all(
        jnp.broadcast_to(own[None], (8, 3, 8 * COLS)), RING_Z, 0, 0, tiled=True
    )
    raw, rows_z = lax.optimization_barrier((inputs[0], rows_z))
    x = exchange(raw)
    act1, slope_x = gelu_parts(x.astype(F32))
    act1 = act1.astype(BF)
    lower1 = jnp.concatenate([along(act1[3 * QUARTER :], 1), act1[: 3 * QUARTER]], axis=0)
    upper1 = jnp.concatenate([act1[QUARTER:], along(act1[:QUARTER], -1)], axis=0)

    rows_x = collect(rows_z.reshape(24, 8 * COLS), "x")
    channels = lax.iota(jnp.int32, ROWS)
    unmix = (slot_owner(-1, False)[None, :] == channels[:, None]).astype(BF)
    mix_one = (slot_owner(1, False)[:, None] == channels[None, :]).astype(BF)
    mix_two = (slot_owner(1, True)[:, None] == channels[None, :]).astype(BF)

    rows_one = collect(rows_x[:, : 4 * COLS], RING_Y)
    rest, rows_one, raw = lax.optimization_barrier((rows_x[:, 4 * COLS :], rows_one, upstream[0]))
    k1 = dot_plain(unmix, collect(rows_one, "core")).astype(BF)
    k2 = dot_plain(unmix, collect(collect(rest, RING_Y), "core")).astype(BF)
    g = exchange(raw)

    def tap(k, i):
        return k[:, i * COLS : (i + 1) * COLS]

    pre1 = (
        dot_plain(act1, tap(k1, 1))
        + dot_plain(lower1, tap(k1, 0))
        + dot_plain(upper1, tap(k1, 2))
    )
    inner1, slope1 = gelu_parts(pre1)
    inner1 = inner1.astype(BF)
    middle = (x.astype(F32) + dot_back(inner1, tap(k1, 3))).astype(BF)

    half = 2 * QUARTER
    act2, slope_m = gelu_parts(middle.astype(F32))
    act2 = act2.astype(BF)
    first, third = dot_plain(act2, tap(k2, 0)), dot_plain(act2, tap(k2, 2))
    to_later = along(first[half:].astype(BF), 1).astype(F32)
    to_earlier = along(third[:half].astype(BF), -1).astype(F32)
    pre2 = (
        dot_plain(act2, tap(k2, 1))
        + jnp.concatenate([to_later, first[:half]], axis=0)
        + jnp.concatenate([third[half:], to_earlier], axis=0)
    )
    inner2, slope2 = gelu_parts(pre2)
    inner2 = inner2.astype(BF)

    dpre2 = (dot_plain(g, tap(k2, 3)) * slope2).astype(BF)
    from_later, from_earlier = along(dpre2[:half], -1), along(dpre2[half:], 1)
    trio2 = jnp.concatenate(
        [
            jnp.concatenate([dpre2[half:], from_later], axis=0),
            dpre2,
            jnp.concatenate([from_earlier, dpre2[:half]], axis=0),
        ],
        axis=1,
    )
    result = exchange((middle.astype(F32) + dot_back(inner2, tap(k2, 3))).astype(BF))

    def core_swap(mix, grads):
        return hop(dot_plain(mix[COLS:], grads).astype(BF), "core", 1)

    def core_sum(mix, grads, got):
        return (dot_plain(mix[:COLS], grads) + got.astype(F32)).astype(BF)

    grads2 = jnp.concatenate([dot_rows(act2, trio2).astype(BF), dot_rows(g, inner2).astype(BF)], axis=1)
    grads2, trio2 = lax.optimization_barrier((grads2, trio2))
    got2 = core_swap(mix_two, grads2)
    dact2 = dot_back(trio2, k2[:, : 3 * COLS])
    middle_grad = (g.astype(F32) + dact2 * slope_m).astype(BF)

    dpre1 = (dot_plain(middle_grad, tap(k1, 3)) * slope1).astype(BF)
    dpre1, got2 = lax.optimization_barrier((dpre1, got2))
    part2 = core_sum(mix_two, grads2, got2)
    grads1 = jnp.concatenate(
        [
            dot_rows(lower1, dpre1).astype(BF),
            dot_rows(act1, dpre1).astype(BF),
            dot_rows(upper1, dpre1).astype(BF),
            dot_rows(middle_grad, inner1).astype(BF),
        ],
        axis=1,
    )
    part1 = core_sum(mix_one, grads1, core_swap(mix_one, grads1))
    trio1 = jnp.concatenate(
        [
            jnp.concatenate([dpre1[QUARTER:], along(dpre1[:QUARTER], -1)], axis=0),
            dpre1,
            jnp.concatenate([along(dpre1[3 * QUARTER :], 1), dpre1[: 3 * QUARTER]], axis=0),
        ],
        axis=1,
    )
    dact1 = dot_back(trio1, k1[:, : 3 * COLS])
    cotangent = exchange((middle_grad.astype(F32) + dact1 * slope_x).astype(BF))

    part2 = spread_sum(spread_sum(part2, "x"), RING_Y)
    part1 = spread_sum(spread_sum(part1, RING_Y), "x")
    both = jnp.concatenate([part1, part2], axis=1).reshape(8, 3, 8 * COLS)
    parts = lax.all_to_all(both, RING_Z, 0, 0, tiled=True)
    wide = jax.ShapeDtypeStruct((3, 3, COLS), BF)
    narrow = jax.ShapeDtypeStruct((3, COLS), BF)
    grads = pl.pallas_call(
        unpack_kernel, out_shape=(wide, narrow, wide, narrow), name="sum_rows"
    )(parts)
    return (result[None], cotangent[None], *grads)


def solution(mesh):
    names = ("yl", "x", "zq", "zp", "yh", "core")
    fine = Mesh(mesh.devices.reshape(2, 4, 4, 2, 2, 2), names)
    seq, batch = names[:4], names[4:]
    specs = (
        P(batch, seq, None),
        P(batch, seq, None),
        P(None, seq + batch, None),
        P(seq + batch, None),
        P(None, seq + batch, None),
        P(seq + batch, None),
    )
    return jax.shard_map(body, mesh=fine, in_specs=specs, out_specs=specs, check_vma=False)
```

```python
import jax
import jax.numpy as jnp
from jax import lax
from jax.experimental import pallas as pl
from jax.experimental.pallas import tpu as pltpu
from jax.sharding import Mesh, PartitionSpec as P

BF = jnp.bfloat16
F32 = jnp.float32
LINE = ("yl", "x")
RING_Y = ("yl", "yh")
COLS = 384
ROWS = 768
QUARTER = 128


def gelu_parts(v):
    cdf = 0.5 * (1.0 + lax.erf(v * 0.7071067811865476))
    slope = cdf + v * jnp.exp(-0.5 * v * v) * 0.3989422804014327
    return v * cdf, slope


def dot_plain(left, right):
    return jnp.dot(left, right, preferred_element_type=F32)


def dot_rows(left, right):
    return lax.dot_general(left, right, (((0,), (0,)), ((), ())), preferred_element_type=F32)


def dot_back(left, right):
    return lax.dot_general(left, right, (((1,), (1,)), ((), ())), preferred_element_type=F32)


def after(value, *others):
    return lax.optimization_barrier((value, *others))[0]


def along(array, by):
    count = lax.axis_size(LINE)
    got = lax.ppermute(array, LINE, [(i, (i + by) % count) for i in range(count)])
    end = 0 if by > 0 else count - 1
    return jnp.where(lax.axis_index(LINE) == end, jnp.zeros_like(got), got)


def permuted(array, axis, target):
    count = lax.axis_size(axis)
    place = (lambda y: y % 2 * 2 + y // 2) if axis == RING_Y else (lambda i: i)
    return lax.ppermute(array, axis, [(place(i), place(target(i) % count)) for i in range(count)])


def hop(array, axis, by):
    return permuted(array, axis, lambda i: i + by)


def swap(array, axis, bits):
    return permuted(array, axis, lambda i: i ^ bits)


def collect(rows, axis):
    count = lax.axis_size(axis)
    return jnp.concatenate([rows] + [hop(rows, axis, k) for k in range(1, count)], axis=0)


def collect_pairs(rows, axis):
    rows = jnp.concatenate([rows, swap(rows, axis, 1)], axis=0)
    if lax.axis_size(axis) == 4:
        rows = jnp.concatenate([rows, swap(rows, axis, 3)], axis=0)
    return rows


def total_of(own, *others):
    total = own.astype(F32)
    for other in others:
        total = total + other.astype(F32)
    return total.astype(BF)


def spread_sum(rows, axis):
    count = lax.axis_size(axis)
    size = rows.shape[0] // count
    got = [hop(rows[k * size : (k + 1) * size], axis, k) for k in range(1, count)]
    return total_of(rows[:size], *got)


def spread_pairs(rows, axis):
    if lax.axis_size(axis) == 4:
        half = rows.shape[0] // 2
        rows = total_of(rows[:half], swap(rows[half:], axis, 3))
    half = rows.shape[0] // 2
    return total_of(rows[:half], swap(rows[half:], axis, 1))


def slot_owner(sign, x_first):
    slot = lax.iota(jnp.int32, ROWS)
    k = lax.div(slot, jnp.int32(3))
    row = slot - 3 * k
    kp, kq, k_in, k_out, kc = k & 1, (k >> 1) & 3, (k >> 3) & 3, (k >> 5) & 3, k >> 7
    zp = lax.axis_index("zp") ^ kp
    zq = lax.axis_index("zq") ^ (kq ^ (kq >> 1))
    x, y = lax.axis_index("x"), lax.axis_index("yh") * 2 + lax.axis_index("yl")
    if x_first:
        y, x = y ^ (k_in ^ (k_in >> 1)), x ^ (k_out ^ (k_out >> 1))
    else:
        x, y = x ^ (k_in ^ (k_in >> 1)), (y + sign * k_out + 4) & 3
    c = lax.axis_index("core") ^ kc
    yh, yl = y >> 1, y & 1
    return ((((yl * 4 + x) * 8 + zq * 2 + zp) * 2 + yh) * 2 + c) * 3 + row


def place_kernel(me, own, first, second, out):
    q = me[0]
    out[q] = own[q]
    out[q ^ 3] = first[q & 1]
    out[q ^ 1] = second[0]
    out[q ^ 2] = second[1]


def exchange(array):
    me = lax.axis_index("zq")
    blocks = array.reshape(4, QUARTER, ROWS)
    first = swap(lax.dynamic_slice_in_dim(blocks, 2 - (me & 2), 2, 0), "zq", 3)
    sent = jnp.concatenate(
        [
            lax.dynamic_slice_in_dim(blocks, me ^ 1, 1, 0),
            lax.dynamic_slice_in_dim(first, 1 - (me & 1), 1, 0),
        ],
        axis=0,
    )
    second = swap(sent, "zq", 1)
    vmem = pl.BlockSpec(memory_space=pltpu.VMEM)
    placed = pl.pallas_call(
        place_kernel,
        in_specs=[pl.BlockSpec(memory_space=pltpu.SMEM), vmem, vmem, vmem],
        out_specs=vmem,
        out_shape=jax.ShapeDtypeStruct((4, QUARTER, ROWS), BF),
        name="place_blocks",
    )(me.reshape(1), blocks, first, second)
    return placed.reshape(4 * QUARTER, ROWS), second


def pack_kernel(wide_one, narrow_one, wide_two, narrow_two, out):
    for at, (wide, narrow) in enumerate(((wide_one, narrow_one), (wide_two, narrow_two))):
        for tap in range(3):
            out[:, (4 * at + tap) * COLS : (4 * at + tap + 1) * COLS] = wide[tap]
        out[:, (4 * at + 3) * COLS : (4 * at + 4) * COLS] = narrow[...]


def unpack_kernel(own, got, wide_one, narrow_one, wide_two, narrow_two):
    total = (own[0].astype(F32) + got[0].astype(F32)).astype(BF)
    for at, (wide, narrow) in enumerate(((wide_one, narrow_one), (wide_two, narrow_two))):
        for tap in range(3):
            wide[tap] = total[:, (4 * at + tap) * COLS : (4 * at + tap + 1) * COLS]
        narrow[...] = total[:, (4 * at + 3) * COLS : (4 * at + 4) * COLS]


def body(inputs, upstream, wide_one, narrow_one, wide_two, narrow_two):
    own = pl.pallas_call(
        pack_kernel, out_shape=jax.ShapeDtypeStruct((3, 8 * COLS), BF), name="pack_rows"
    )(wide_one, narrow_one, wide_two, narrow_two)
    rows_z = collect_pairs(collect_pairs(own, "zp"), "zq")
    raw, rows_z = lax.optimization_barrier((inputs[0], rows_z))
    rows_one = collect_pairs(rows_z[:, : 4 * COLS], "x")
    rows_two = collect_pairs(rows_z[:, 4 * COLS :], RING_Y)
    x, arrived = exchange(raw)
    act1, slope_x = gelu_parts(x.astype(F32))
    act1 = act1.astype(BF)
    lower1 = jnp.concatenate([along(act1[3 * QUARTER :], 1), act1[: 3 * QUARTER]], axis=0)
    upper1 = jnp.concatenate([act1[QUARTER:], along(act1[:QUARTER], -1)], axis=0)

    channels = lax.iota(jnp.int32, ROWS)

    def unmixed(rows, x_first):
        return dot_plain((slot_owner(-1, x_first)[None, :] == channels[:, None]).astype(BF), rows).astype(BF)

    mix_one = (slot_owner(1, False)[:, None] == channels[None, :]).astype(BF)
    mix_two = (slot_owner(1, True)[:, None] == channels[None, :]).astype(BF)

    rows_one = collect(rows_one, RING_Y)
    rows_two = collect_pairs(rows_two, "x")
    k1 = unmixed(collect_pairs(rows_one, "core"), False)
    rows_two = collect_pairs(rows_two, "core")
    g, _ = exchange(after(upstream[0], arrived))

    def tap(k, i):
        return k[:, i * COLS : (i + 1) * COLS]

    pre1 = (
        dot_plain(act1, tap(k1, 1))
        + dot_plain(lower1, tap(k1, 0))
        + dot_plain(upper1, tap(k1, 2))
    )
    inner1, slope1 = gelu_parts(pre1)
    inner1 = inner1.astype(BF)
    middle = (x.astype(F32) + dot_back(inner1, tap(k1, 3))).astype(BF)
    k2 = unmixed(after(rows_two, middle), True)

    half = 2 * QUARTER
    act2, slope_m = gelu_parts(middle.astype(F32))
    act2 = act2.astype(BF)
    first, third = dot_plain(act2, tap(k2, 0)), dot_plain(act2, tap(k2, 2))
    to_later = along(first[half:].astype(BF), 1).astype(F32)
    to_earlier = along(third[:half].astype(BF), -1).astype(F32)
    pre2 = (
        dot_plain(act2, tap(k2, 1))
        + jnp.concatenate([to_later, first[:half]], axis=0)
        + jnp.concatenate([third[half:], to_earlier], axis=0)
    )
    inner2, slope2 = gelu_parts(pre2)
    inner2 = inner2.astype(BF)

    dpre2 = (dot_plain(g, tap(k2, 3)) * slope2).astype(BF)
    from_later, from_earlier = along(dpre2[:half], -1), along(dpre2[half:], 1)
    trio2 = jnp.concatenate(
        [
            jnp.concatenate([dpre2[half:], from_later], axis=0),
            dpre2,
            jnp.concatenate([from_earlier, dpre2[:half]], axis=0),
        ],
        axis=1,
    )
    grads2 = jnp.concatenate([dot_rows(act2, trio2).astype(BF), dot_rows(g, inner2).astype(BF)], axis=1)
    sent2 = dot_plain(mix_two[COLS:], grads2).astype(BF)
    got2 = swap(sent2, "core", 1)
    trio2 = after(trio2, sent2)
    dact2 = dot_back(trio2, k2[:, : 3 * COLS])
    middle_grad = (g.astype(F32) + dact2 * slope_m).astype(BF)

    dpre1 = (dot_plain(middle_grad, tap(k1, 3)) * slope1).astype(BF)
    grads1 = jnp.concatenate(
        [
            dot_rows(lower1, dpre1).astype(BF),
            dot_rows(act1, dpre1).astype(BF),
            dot_rows(upper1, dpre1).astype(BF),
            dot_rows(middle_grad, inner1).astype(BF),
        ],
        axis=1,
    )
    sent1 = dot_plain(mix_one[COLS:], grads1).astype(BF)
    got1 = swap(sent1, "core", 1)
    dpre1, grads1, grads2, got2, inner2, _ = lax.optimization_barrier(
        (dpre1, grads1, grads2, got2, inner2, sent1)
    )
    kept1 = dot_plain(mix_one[:COLS], grads1).astype(BF)
    kept2 = dot_plain(mix_two[:COLS], grads2).astype(BF)
    trio1 = jnp.concatenate(
        [
            jnp.concatenate([dpre1[QUARTER:], along(dpre1[:QUARTER], -1)], axis=0),
            dpre1,
            jnp.concatenate([along(dpre1[3 * QUARTER :], 1), dpre1[: 3 * QUARTER]], axis=0),
        ],
        axis=1,
    )
    result, _ = exchange((middle.astype(F32) + dot_back(inner2, tap(k2, 3))).astype(BF))
    part1 = spread_sum(total_of(kept1, got1), RING_Y)
    part2 = spread_pairs(total_of(kept2, got2), "x")
    dact1 = dot_back(trio1, k1[:, : 3 * COLS])
    cotangent, _ = exchange((middle_grad.astype(F32) + dact1 * slope_x).astype(BF))

    part1 = spread_pairs(part1, "x")
    part2 = spread_pairs(part2, RING_Y)
    both = jnp.concatenate([part1, part2], axis=1).reshape(8, 3, 8 * COLS)
    both = spread_pairs(both, "zq")
    wide = jax.ShapeDtypeStruct((3, 3, COLS), BF)
    narrow = jax.ShapeDtypeStruct((3, COLS), BF)
    grads = pl.pallas_call(
        unpack_kernel, out_shape=(wide, narrow, wide, narrow), name="sum_rows"
    )(both[:1], swap(both[1:], "zp", 1))
    return (result[None], cotangent[None], *grads)


def solution(mesh):
    names = ("yl", "x", "zq", "zp", "yh", "core")
    fine = Mesh(mesh.devices.reshape(2, 4, 4, 2, 2, 2), names)
    seq, batch = names[:4], names[4:]
    specs = (
        P(batch, seq, None),
        P(batch, seq, None),
        P(None, seq + batch, None),
        P(seq + batch, None),
        P(None, seq + batch, None),
        P(seq + batch, None),
    )
    return jax.shard_map(body, mesh=fine, in_specs=specs, out_specs=specs, check_vma=False)
```

```python
import jax
import jax.numpy as jnp
from jax import lax
from jax.experimental import pallas as pl
from jax.experimental.pallas import tpu as pltpu
from jax.sharding import Mesh, PartitionSpec as P

BF = jnp.bfloat16
F32 = jnp.float32
LINE = ("yl", "x")
RING_Y = ("yl", "yh")
COLS = 384
ROWS = 768
QUARTER = 128


def gelu_parts(v):
    cdf = 0.5 * (1.0 + lax.erf(v * 0.7071067811865476))
    slope = cdf + v * jnp.exp(-0.5 * v * v) * 0.3989422804014327
    return v * cdf, slope


def dot_plain(left, right):
    return jnp.dot(left, right, preferred_element_type=F32)


def dot_rows(left, right):
    return lax.dot_general(left, right, (((0,), (0,)), ((), ())), preferred_element_type=F32)


def dot_back(left, right):
    return lax.dot_general(left, right, (((1,), (1,)), ((), ())), preferred_element_type=F32)


def after(value, *others):
    return lax.optimization_barrier((value, *others))[0]


def along(array, by):
    count = lax.axis_size(LINE)
    got = lax.ppermute(array, LINE, [(i, (i + by) % count) for i in range(count)])
    end = 0 if by > 0 else count - 1
    return jnp.where(lax.axis_index(LINE) == end, jnp.zeros_like(got), got)


def permuted(array, axis, target):
    count = lax.axis_size(axis)
    place = (lambda y: y % 2 * 2 + y // 2) if axis == RING_Y else (lambda i: i)
    return lax.ppermute(array, axis, [(place(i), place(target(i) % count)) for i in range(count)])


def hop(array, axis, by):
    return permuted(array, axis, lambda i: i + by)


def swap(array, axis, bits):
    return permuted(array, axis, lambda i: i ^ bits)


def collect(rows, axis):
    count = lax.axis_size(axis)
    return jnp.concatenate([rows] + [hop(rows, axis, k) for k in range(1, count)], axis=0)


def collect_pairs(rows, axis):
    rows = jnp.concatenate([rows, swap(rows, axis, 1)], axis=0)
    if lax.axis_size(axis) == 4:
        rows = jnp.concatenate([rows, swap(rows, axis, 3)], axis=0)
    return rows


def total_of(own, *others):
    total = own.astype(F32)
    for other in others:
        total = total + other.astype(F32)
    return total.astype(BF)


def spread(rows, axis):
    count = lax.axis_size(axis)
    size = rows.shape[0] // count
    return [rows[:size]] + [hop(rows[k * size : (k + 1) * size], axis, k) for k in range(1, count)]


def spread_half(rows, axis, bits):
    half = rows.shape[0] // 2
    return rows[:half], swap(rows[half:], axis, bits)


def spread_pairs(rows, axis):
    return total_of(*spread_half(total_of(*spread_half(rows, axis, 3)), axis, 1))


def slot_owner(sign, x_first):
    slot = lax.iota(jnp.int32, ROWS)
    k = lax.div(slot, jnp.int32(3))
    row = slot - 3 * k
    kp, kq, k_in, k_out, kc = k & 1, (k >> 1) & 3, (k >> 3) & 3, (k >> 5) & 3, k >> 7
    zp = lax.axis_index("zp") ^ kp
    zq = lax.axis_index("zq") ^ (kq ^ (kq >> 1))
    x, y = lax.axis_index("x"), lax.axis_index("yh") * 2 + lax.axis_index("yl")
    if x_first:
        y, x = y ^ (k_in ^ (k_in >> 1)), x ^ (k_out ^ (k_out >> 1))
    else:
        x, y = x ^ (k_in ^ (k_in >> 1)), (y + sign * k_out + 4) & 3
    c = lax.axis_index("core") ^ kc
    yh, yl = y >> 1, y & 1
    return ((((yl * 4 + x) * 8 + zq * 2 + zp) * 2 + yh) * 2 + c) * 3 + row


def piece_of(array, k):
    me = lax.axis_index("zq")
    sent = lax.dynamic_slice_in_dim(array, ((me + k) & 3) * QUARTER, QUARTER, 0)
    return hop(sent, "zq", k), ((me + 4 - k) & 3) * QUARTER


def placed(array, pieces):
    for piece, at in pieces:
        array = lax.dynamic_update_slice_in_dim(array, piece, at, 0)
    return array


def pack_kernel(wide_one, narrow_one, wide_two, narrow_two, out):
    for at, (wide, narrow) in enumerate(((wide_one, narrow_one), (wide_two, narrow_two))):
        for tap in range(3):
            out[:, (4 * at + tap) * COLS : (4 * at + tap + 1) * COLS] = wide[tap]
        out[:, (4 * at + 3) * COLS : (4 * at + 4) * COLS] = narrow[...]


def unpack_kernel(own, got, wide_one, narrow_one, wide_two, narrow_two):
    total = (own[0].astype(F32) + got[0].astype(F32)).astype(BF)
    for at, (wide, narrow) in enumerate(((wide_one, narrow_one), (wide_two, narrow_two))):
        for tap in range(3):
            wide[tap] = total[:, (4 * at + tap) * COLS : (4 * at + tap + 1) * COLS]
        narrow[...] = total[:, (4 * at + 3) * COLS : (4 * at + 4) * COLS]


def body(inputs, upstream, wide_one, narrow_one, wide_two, narrow_two):
    own = pl.pallas_call(
        pack_kernel, out_shape=jax.ShapeDtypeStruct((3, 8 * COLS), BF), name="pack_rows"
    )(wide_one, narrow_one, wide_two, narrow_two)
    rows_z = collect_pairs(collect_pairs(own, "zp"), "zq")
    raw, rows_z = lax.optimization_barrier((inputs[0], rows_z))
    next_x, last_x, far_x = piece_of(raw, 1), piece_of(raw, 3), piece_of(raw, 2)
    rows_one = collect_pairs(rows_z[:, : 4 * COLS], "x")
    rows_two = collect_pairs(rows_z[:, 4 * COLS :], RING_Y)
    rows_one = collect(after(rows_one, next_x[0]), RING_Y)
    rows_one = after(rows_one, last_x[0], far_x[0])
    x = placed(raw, (next_x, last_x, far_x))
    raw = after(upstream[0], far_x[0])
    next_g = piece_of(raw, 1)
    act1, slope_x = gelu_parts(x.astype(F32))
    act1 = act1.astype(BF)
    lower1 = jnp.concatenate([along(act1[3 * QUARTER :], 1), act1[: 3 * QUARTER]], axis=0)
    upper1 = jnp.concatenate([act1[QUARTER:], along(act1[:QUARTER], -1)], axis=0)

    channels = lax.iota(jnp.int32, ROWS)

    def unmixed(rows, x_first):
        return dot_plain((slot_owner(-1, x_first)[None, :] == channels[:, None]).astype(BF), rows).astype(BF)

    mix_one = (slot_owner(1, False)[:, None] == channels[None, :]).astype(BF)
    mix_two = (slot_owner(1, True)[:, None] == channels[None, :]).astype(BF)

    rows_two = collect_pairs(rows_two, "x")
    k1 = unmixed(collect_pairs(rows_one, "core"), False)
    last_g = piece_of(after(raw, k1), 3)
    rows_two = collect_pairs(rows_two, "core")

    def tap(k, i):
        return k[:, i * COLS : (i + 1) * COLS]

    pre1 = (
        dot_plain(act1, tap(k1, 1))
        + dot_plain(lower1, tap(k1, 0))
        + dot_plain(upper1, tap(k1, 2))
    )
    inner1, slope1 = gelu_parts(pre1)
    inner1 = inner1.astype(BF)
    middle = (x.astype(F32) + dot_back(inner1, tap(k1, 3))).astype(BF)
    k2 = unmixed(after(rows_two, middle), True)

    half = 2 * QUARTER
    act2, slope_m = gelu_parts(middle.astype(F32))
    act2 = act2.astype(BF)
    first, third = dot_plain(act2, tap(k2, 0)), dot_plain(act2, tap(k2, 2))
    to_later = along(first[half:].astype(BF), 1).astype(F32)
    to_earlier = along(third[:half].astype(BF), -1).astype(F32)
    far_g = piece_of(after(raw, first), 2)
    pre2 = (
        dot_plain(act2, tap(k2, 1))
        + jnp.concatenate([to_later, first[:half]], axis=0)
        + jnp.concatenate([third[half:], to_earlier], axis=0)
    )
    inner2, slope2 = gelu_parts(pre2)
    inner2 = inner2.astype(BF)
    g = placed(raw, (next_g, last_g, far_g))

    dpre2 = (dot_plain(g, tap(k2, 3)) * slope2).astype(BF)
    from_later, from_earlier = along(dpre2[:half], -1), along(dpre2[half:], 1)
    trio2 = jnp.concatenate(
        [
            jnp.concatenate([dpre2[half:], from_later], axis=0),
            dpre2,
            jnp.concatenate([from_earlier, dpre2[:half]], axis=0),
        ],
        axis=1,
    )
    result = middle.astype(F32) + dot_back(after(inner2, from_later), tap(k2, 3))
    result = result.astype(BF)
    next_r, last_r = piece_of(result, 1), piece_of(result, 3)
    grads2 = jnp.concatenate([dot_rows(act2, trio2).astype(BF), dot_rows(g, inner2).astype(BF)], axis=1)
    sent2 = dot_plain(mix_two[COLS:], grads2).astype(BF)
    got2 = swap(sent2, "core", 1)
    trio2 = after(trio2, sent2)
    dact2 = dot_back(trio2, k2[:, : 3 * COLS])
    middle_grad = (g.astype(F32) + dact2 * slope_m).astype(BF)

    dpre1 = (dot_plain(middle_grad, tap(k1, 3)) * slope1).astype(BF)
    dpre1, got2 = lax.optimization_barrier((dpre1, got2))
    part2 = total_of(dot_plain(mix_two[:COLS], grads2).astype(BF), got2)
    dpre1 = after(dpre1, part2, next_r[0], last_r[0])
    grads1 = jnp.concatenate(
        [
            dot_rows(lower1, dpre1).astype(BF),
            dot_rows(act1, dpre1).astype(BF),
            dot_rows(upper1, dpre1).astype(BF),
            dot_rows(middle_grad, inner1).astype(BF),
        ],
        axis=1,
    )
    sent1 = dot_plain(mix_one[COLS:], grads1).astype(BF)
    got1 = swap(sent1, "core", 1)
    dpre1, grads1, sent1 = lax.optimization_barrier((dpre1, grads1, sent1))
    kept1 = dot_plain(mix_one[:COLS], grads1).astype(BF)
    trio1 = jnp.concatenate(
        [
            jnp.concatenate([dpre1[QUARTER:], along(dpre1[:QUARTER], -1)], axis=0),
            dpre1,
            jnp.concatenate([along(dpre1[3 * QUARTER :], 1), dpre1[: 3 * QUARTER]], axis=0),
        ],
        axis=1,
    )
    part1 = total_of(kept1, got1)
    trio1, result, part1 = lax.optimization_barrier((trio1, result, part1))
    far_r = piece_of(result, 2)
    part1 = spread(part1, RING_Y)
    near2, far2 = spread_half(part2, "x", 3)
    dact1 = dot_back(trio1, k1[:, : 3 * COLS])
    cotangent = (middle_grad.astype(F32) + dact1 * slope_x).astype(BF)
    cotangent, far2, part1[1] = lax.optimization_barrier((cotangent, far2, part1[1]))
    part2 = total_of(*spread_half(total_of(near2, far2), "x", 1))
    pieces = [piece_of(cotangent, k) for k in (1, 3, 2)]
    cotangent = placed(cotangent, pieces)

    part1 = after(total_of(*part1), far_r[0])
    result = placed(result, (next_r, last_r, far_r))
    part1 = spread_pairs(part1, "x")
    part2 = spread_pairs(part2, RING_Y)
    both = jnp.concatenate([part1, part2], axis=1).reshape(8, 3, 8 * COLS)
    both = spread_pairs(both, "zq")
    wide = jax.ShapeDtypeStruct((3, 3, COLS), BF)
    narrow = jax.ShapeDtypeStruct((3, COLS), BF)
    grads = pl.pallas_call(
        unpack_kernel, out_shape=(wide, narrow, wide, narrow), name="sum_rows"
    )(both[:1], swap(both[1:], "zp", 1))
    return (result[None], cotangent[None], *grads)


def solution(mesh):
    names = ("yl", "x", "zq", "zp", "yh", "core")
    fine = Mesh(mesh.devices.reshape(2, 4, 4, 2, 2, 2), names)
    seq, batch = names[:4], names[4:]
    specs = (
        P(batch, seq, None),
        P(batch, seq, None),
        P(None, seq + batch, None),
        P(seq + batch, None),
        P(None, seq + batch, None),
        P(seq + batch, None),
    )
    return jax.shard_map(body, mesh=fine, in_specs=specs, out_specs=specs, check_vma=False)
```

```python
import jax
import jax.numpy as jnp
from jax import lax
from jax.experimental import pallas as pl
from jax.experimental.pallas import tpu as pltpu
from jax.sharding import Mesh, PartitionSpec as P

BF = jnp.bfloat16
F32 = jnp.float32
LINE = ("yl", "x")
RING_Y = ("yl", "yh")
COLS = 384
ROWS = 768
QUARTER = 128


def gelu_parts(v):
    cdf = 0.5 * (1.0 + lax.erf(v * 0.7071067811865476))
    slope = cdf + v * jnp.exp(-0.5 * v * v) * 0.3989422804014327
    return v * cdf, slope


def dot_plain(left, right):
    return jnp.dot(left, right, preferred_element_type=F32)


def dot_rows(left, right):
    return lax.dot_general(left, right, (((0,), (0,)), ((), ())), preferred_element_type=F32)


def dot_back(left, right):
    return lax.dot_general(left, right, (((1,), (1,)), ((), ())), preferred_element_type=F32)


def after(value, *others):
    return lax.optimization_barrier((value, *others))[0]


def along(array, by):
    count = lax.axis_size(LINE)
    got = lax.ppermute(array, LINE, [(i, (i + by) % count) for i in range(count)])
    end = 0 if by > 0 else count - 1
    return jnp.where(lax.axis_index(LINE) == end, jnp.zeros_like(got), got)


def permuted(array, axis, target):
    count = lax.axis_size(axis)
    place = (lambda y: y % 2 * 2 + y // 2) if axis == RING_Y else (lambda i: i)
    return lax.ppermute(array, axis, [(place(i), place(target(i) % count)) for i in range(count)])


def hop(array, axis, by):
    return permuted(array, axis, lambda i: i + by)


def swap(array, axis, bits):
    return permuted(array, axis, lambda i: i ^ bits)


def collect(rows, axis):
    count = lax.axis_size(axis)
    return jnp.concatenate([rows] + [hop(rows, axis, k) for k in range(1, count)], axis=0)


def collect_pairs(rows, axis):
    rows = jnp.concatenate([rows, swap(rows, axis, 1)], axis=0)
    if lax.axis_size(axis) == 4:
        rows = jnp.concatenate([rows, swap(rows, axis, 3)], axis=0)
    return rows


def total_of(own, *others):
    total = own.astype(F32)
    for other in others:
        total = total + other.astype(F32)
    return total.astype(BF)


def spread(rows, axis):
    count = lax.axis_size(axis)
    size = rows.shape[0] // count
    return [rows[:size]] + [hop(rows[k * size : (k + 1) * size], axis, k) for k in range(1, count)]


def spread_half(rows, axis, bits):
    half = rows.shape[0] // 2
    return rows[:half], swap(rows[half:], axis, bits)


def spread_pairs(rows, axis):
    return total_of(*spread_half(total_of(*spread_half(rows, axis, 3)), axis, 1))


def slot_owner(sign, x_first):
    slot = lax.iota(jnp.int32, ROWS)
    k = lax.div(slot, jnp.int32(3))
    row = slot - 3 * k
    kp, kq, k_in, k_out, kc = k & 1, (k >> 1) & 3, (k >> 3) & 3, (k >> 5) & 3, k >> 7
    zp = lax.axis_index("zp") ^ kp
    zq = (lax.axis_index("zq") + sign * kq + 4) & 3
    x, y = lax.axis_index("x"), lax.axis_index("yh") * 2 + lax.axis_index("yl")
    if x_first:
        y = y ^ (k_in ^ (k_in >> 1))
        x = x ^ (k_out ^ (k_out >> 1)) if sign > 0 else (x - k_out + 4) & 3
    else:
        x = x ^ (k_in ^ (k_in >> 1))
        y = y ^ (k_out ^ (k_out >> 1)) if sign > 0 else (y - k_out + 4) & 3
    c = lax.axis_index("core") ^ kc
    yh, yl = y >> 1, y & 1
    return ((((yl * 4 + x) * 8 + zq * 2 + zp) * 2 + yh) * 2 + c) * 3 + row


def piece_of(array, k):
    me = lax.axis_index("zq")
    sent = lax.dynamic_slice_in_dim(array, ((me + k) & 3) * QUARTER, QUARTER, 0)
    return hop(sent, "zq", k), ((me + 4 - k) & 3) * QUARTER


def place_kernel(me, own, first, second, out):
    q = me[0]
    out[q] = own[q]
    out[q ^ 3] = first[q & 1]
    out[q ^ 1] = second[0]
    out[q ^ 2] = second[1]


def exchange_first(array):
    me = lax.axis_index("zq")
    blocks = array.reshape(4, QUARTER, ROWS)
    return blocks, swap(lax.dynamic_slice_in_dim(blocks, 2 - (me & 2), 2, 0), "zq", 3)


def exchange_second(blocks, first):
    me = lax.axis_index("zq")
    sent = jnp.concatenate(
        [
            lax.dynamic_slice_in_dim(blocks, me ^ 1, 1, 0),
            lax.dynamic_slice_in_dim(first, 1 - (me & 1), 1, 0),
        ],
        axis=0,
    )
    second = swap(sent, "zq", 1)
    vmem = pl.BlockSpec(memory_space=pltpu.VMEM)
    result = pl.pallas_call(
        place_kernel,
        in_specs=[pl.BlockSpec(memory_space=pltpu.SMEM), vmem, vmem, vmem],
        out_specs=vmem,
        out_shape=jax.ShapeDtypeStruct((4, QUARTER, ROWS), BF),
        name="place_blocks",
    )(me.reshape(1), blocks, first, second)
    return second, result.reshape(4 * QUARTER, ROWS)


def placed(array, pieces):
    for piece, at in pieces:
        array = lax.dynamic_update_slice_in_dim(array, piece, at, 0)
    return array


def pack_kernel(wide_one, narrow_one, wide_two, narrow_two, out):
    for at, (wide, narrow) in enumerate(((wide_one, narrow_one), (wide_two, narrow_two))):
        for tap in range(3):
            out[:, (4 * at + tap) * COLS : (4 * at + tap + 1) * COLS] = wide[tap]
        out[:, (4 * at + 3) * COLS : (4 * at + 4) * COLS] = narrow[...]


def unpack_kernel(own, got, wide_one, narrow_one, wide_two, narrow_two):
    total = (own[0].astype(F32) + got[0].astype(F32)).astype(BF)
    for at, (wide, narrow) in enumerate(((wide_one, narrow_one), (wide_two, narrow_two))):
        for tap in range(3):
            wide[tap] = total[:, (4 * at + tap) * COLS : (4 * at + tap + 1) * COLS]
        narrow[...] = total[:, (4 * at + 3) * COLS : (4 * at + 4) * COLS]


def body(inputs, upstream, wide_one, narrow_one, wide_two, narrow_two):
    own = pl.pallas_call(
        pack_kernel, out_shape=jax.ShapeDtypeStruct((3, 8 * COLS), BF), name="pack_rows"
    )(wide_one, narrow_one, wide_two, narrow_two)
    raw = inputs[0]
    next_x, last_x, far_x = piece_of(raw, 1), piece_of(raw, 3), piece_of(raw, 2)
    rows_z = collect_pairs(own, "zp")
    rows_z = collect(after(rows_z, next_x[0]), "zq")
    rows_z = after(rows_z, last_x[0])
    rows_one, rows_two = rows_z[:, : 4 * COLS], rows_z[:, 4 * COLS :]
    rows_one = jnp.concatenate([rows_one, swap(rows_one, "x", 1)], axis=0)
    rows_two = jnp.concatenate([rows_two, swap(rows_two, RING_Y, 1)], axis=0)
    rows_one, rows_two = after(rows_one, far_x[0]), after(rows_two, far_x[0])
    rows_one = jnp.concatenate([rows_one, swap(rows_one, "x", 3)], axis=0)
    rows_two = jnp.concatenate([rows_two, swap(rows_two, RING_Y, 3)], axis=0)
    x = placed(raw, (next_x, last_x, far_x))
    act1, slope_x = gelu_parts(x.astype(F32))
    act1 = act1.astype(BF)
    below, above = along(act1[3 * QUARTER :], 1), along(act1[:QUARTER], -1)
    lower1 = jnp.concatenate([below, act1[: 3 * QUARTER]], axis=0)
    upper1 = jnp.concatenate([act1[QUARTER:], above], axis=0)
    rows_one = collect(after(rows_one, below, above, rows_two), RING_Y)
    raw = after(upstream[0], rows_one)
    next_g = piece_of(raw, 1)

    channels = lax.iota(jnp.int32, ROWS)

    def unmixed(rows, x_first):
        return dot_plain((slot_owner(-1, x_first)[None, :] == channels[:, None]).astype(BF), rows).astype(BF)

    mix_one = (slot_owner(1, False)[:, None] == channels[None, :]).astype(BF)
    mix_two = (slot_owner(1, True)[:, None] == channels[None, :]).astype(BF)

    far_two, next_two = hop(rows_two, "x", 2), hop(rows_two, "x", 1)
    k1 = unmixed(collect_pairs(rows_one, "core"), False)
    last_two = hop(after(rows_two, k1), "x", 3)
    rows_two = jnp.concatenate([rows_two, next_two, far_two, last_two], axis=0)
    last_g = piece_of(after(raw, k1), 3)

    def tap(k, i):
        return k[:, i * COLS : (i + 1) * COLS]

    pre1 = (
        dot_plain(act1, tap(k1, 1))
        + dot_plain(lower1, tap(k1, 0))
        + dot_plain(upper1, tap(k1, 2))
    )
    inner1, slope1 = gelu_parts(pre1)
    inner1 = inner1.astype(BF)
    middle = (x.astype(F32) + dot_back(inner1, tap(k1, 3))).astype(BF)
    k2 = unmixed(collect_pairs(after(rows_two, middle), "core"), True)

    half = 2 * QUARTER
    act2, slope_m = gelu_parts(middle.astype(F32))
    act2 = act2.astype(BF)
    first, third = dot_plain(act2, tap(k2, 0)), dot_plain(act2, tap(k2, 2))
    to_later = along(first[half:].astype(BF), 1).astype(F32)
    to_earlier = along(third[:half].astype(BF), -1).astype(F32)
    far_g = piece_of(after(raw, first), 2)
    pre2 = (
        dot_plain(act2, tap(k2, 1))
        + jnp.concatenate([to_later, first[:half]], axis=0)
        + jnp.concatenate([third[half:], to_earlier], axis=0)
    )
    inner2, slope2 = gelu_parts(pre2)
    inner2 = inner2.astype(BF)
    g = placed(raw, (next_g, last_g, far_g))

    dpre2 = (dot_plain(g, tap(k2, 3)) * slope2).astype(BF)
    from_later, from_earlier = along(dpre2[:half], -1), along(dpre2[half:], 1)
    trio2 = jnp.concatenate(
        [
            jnp.concatenate([dpre2[half:], from_later], axis=0),
            dpre2,
            jnp.concatenate([from_earlier, dpre2[:half]], axis=0),
        ],
        axis=1,
    )
    grads2 = jnp.concatenate([dot_rows(act2, trio2).astype(BF), dot_rows(g, inner2).astype(BF)], axis=1)
    sent2 = dot_plain(mix_two[COLS:], grads2).astype(BF)
    got2 = swap(sent2, "core", 1)
    trio2 = after(trio2, sent2)
    dact2 = dot_back(trio2, k2[:, : 3 * COLS])
    middle_grad = (g.astype(F32) + dact2 * slope_m).astype(BF)

    dpre1 = (dot_plain(middle_grad, tap(k1, 3)) * slope1).astype(BF)
    dpre1 = after(dpre1, got2)
    part2 = total_of(dot_plain(mix_two[:COLS], grads2).astype(BF), got2)
    near2, far2 = spread_half(part2, "x", 3)
    trio1 = jnp.concatenate(
        [
            jnp.concatenate([dpre1[QUARTER:], along(dpre1[:QUARTER], -1)], axis=0),
            dpre1,
            jnp.concatenate([along(dpre1[3 * QUARTER :], 1), dpre1[: 3 * QUARTER]], axis=0),
        ],
        axis=1,
    )
    dpre1 = after(dpre1, part2)
    grads1 = jnp.concatenate(
        [
            dot_rows(lower1, dpre1).astype(BF),
            dot_rows(act1, dpre1).astype(BF),
            dot_rows(upper1, dpre1).astype(BF),
            dot_rows(middle_grad, inner1).astype(BF),
        ],
        axis=1,
    )
    sent1 = dot_plain(mix_one[COLS:], grads1).astype(BF)
    got1 = swap(sent1, "core", 1)
    kept1 = dot_plain(mix_one[:COLS], after(grads1, sent1)).astype(BF)
    part1 = total_of(kept1, got1)
    dact1 = dot_back(after(trio1, sent1), k1[:, : 3 * COLS])
    cotangent = (middle_grad.astype(F32) + dact1 * slope_x).astype(BF)
    blocks_c, first_c = exchange_first(cotangent)
    result = middle.astype(F32) + dot_back(after(inner2, part1), tap(k2, 3))
    blocks_r, first_r = exchange_first(result.astype(BF))
    part1 = spread_half(part1, RING_Y, 3)
    part2 = total_of(*spread_half(total_of(near2, after(far2, part1[1])), "x", 1))
    second_c, cotangent = exchange_second(blocks_c, after(first_c, part1[1]))
    part1 = spread_half(total_of(*part1), RING_Y, 1)
    second_r, result = exchange_second(blocks_r, after(first_r, part1[1]))
    part1 = spread_pairs(total_of(*part1), "x")
    part2 = spread_pairs(part2, RING_Y)
    both = jnp.concatenate([part1, part2], axis=1).reshape(8, 3, 8 * COLS)
    both = after(total_of(*spread(both, "zq")), second_c, second_r)
    wide = jax.ShapeDtypeStruct((3, 3, COLS), BF)
    narrow = jax.ShapeDtypeStruct((3, COLS), BF)
    grads = pl.pallas_call(
        unpack_kernel, out_shape=(wide, narrow, wide, narrow), name="sum_rows"
    )(both[:1], swap(both[1:], "zp", 1))
    return (result[None], cotangent[None], *grads)


def solution(mesh):
    names = ("yl", "x", "zq", "zp", "yh", "core")
    fine = Mesh(mesh.devices.reshape(2, 4, 4, 2, 2, 2), names)
    seq, batch = names[:4], names[4:]
    specs = (
        P(batch, seq, None),
        P(batch, seq, None),
        P(None, seq + batch, None),
        P(seq + batch, None),
        P(None, seq + batch, None),
        P(seq + batch, None),
    )
    return jax.shard_map(body, mesh=fine, in_specs=specs, out_specs=specs, check_vma=False)
```

```python
import jax
import jax.numpy as jnp
from jax import lax
from jax.experimental import pallas as pl
from jax.experimental.pallas import tpu as pltpu
from jax.sharding import Mesh, PartitionSpec as P

BF = jnp.bfloat16
F32 = jnp.float32
LINE = ("yl", "x")
RING_Y = ("yl", "yh")
RING_Z = ("zq", "zp")
COLS = 384
ROWS = 768
QUARTER = 128


def gelu_parts(v):
    cdf = 0.5 * (1.0 + lax.erf(v * 0.7071067811865476))
    slope = cdf + v * jnp.exp(-0.5 * v * v) * 0.3989422804014327
    return v * cdf, slope


def dot_plain(left, right):
    return jnp.dot(left, right, preferred_element_type=F32)


def dot_rows(left, right):
    return lax.dot_general(left, right, (((0,), (0,)), ((), ())), preferred_element_type=F32)


def dot_back(left, right):
    return lax.dot_general(left, right, (((1,), (1,)), ((), ())), preferred_element_type=F32)


def after(value, *others):
    return lax.optimization_barrier((value, *others))[0]


def along(array, by):
    count = lax.axis_size(LINE)
    got = lax.ppermute(array, LINE, [(i, (i + by) % count) for i in range(count)])
    end = 0 if by > 0 else count - 1
    return jnp.where(lax.axis_index(LINE) == end, jnp.zeros_like(got), got)


def permuted(array, axis, target):
    count = lax.axis_size(axis)
    place = (lambda y: y % 2 * 2 + y // 2) if axis == RING_Y else (lambda i: i)
    return lax.ppermute(array, axis, [(place(i), place(target(i) % count)) for i in range(count)])


def hop(array, axis, by):
    return permuted(array, axis, lambda i: i + by)


def swap(array, axis, bits):
    return permuted(array, axis, lambda i: i ^ bits)


def collect(rows, axis):
    count = lax.axis_size(axis)
    return jnp.concatenate([rows] + [hop(rows, axis, k) for k in range(1, count)], axis=0)


def collect_pairs(rows, axis):
    rows = jnp.concatenate([rows, swap(rows, axis, 1)], axis=0)
    if lax.axis_size(axis) == 4:
        rows = jnp.concatenate([rows, swap(rows, axis, 3)], axis=0)
    return rows


def total_of(own, *others):
    total = own.astype(F32)
    for other in others:
        total = total + other.astype(F32)
    return total.astype(BF)


def spread(rows, axis):
    count = lax.axis_size(axis)
    size = rows.shape[0] // count
    return [rows[:size]] + [hop(rows[k * size : (k + 1) * size], axis, k) for k in range(1, count)]


def spread_half(rows, axis, bits):
    half = rows.shape[0] // 2
    return rows[:half], swap(rows[half:], axis, bits)


def spread_pairs(rows, axis):
    return total_of(*spread_half(total_of(*spread_half(rows, axis, 3)), axis, 1))


def slot_owner(sign, x_first):
    slot = lax.iota(jnp.int32, ROWS)
    k = lax.div(slot, jnp.int32(3))
    row = slot - 3 * k
    kp, kq, k_in, k_out, kc = k & 1, (k >> 1) & 3, (k >> 3) & 3, (k >> 5) & 3, k >> 7
    zp, zq = kp, kq
    if sign > 0:
        zp, zq = lax.axis_index("zp") ^ kp, lax.axis_index("zq") ^ (kq ^ (kq >> 1))
    x, y = lax.axis_index("x"), lax.axis_index("yh") * 2 + lax.axis_index("yl")
    if x_first:
        y = y ^ (k_in ^ (k_in >> 1))
        x = x ^ (k_out ^ (k_out >> 1)) if sign > 0 else (x - k_out + 4) & 3
    else:
        x, y = x ^ (k_in ^ (k_in >> 1)), (y + sign * k_out + 4) & 3
    c = lax.axis_index("core") ^ kc
    yh, yl = y >> 1, y & 1
    return ((((yl * 4 + x) * 8 + zq * 2 + zp) * 2 + yh) * 2 + c) * 3 + row


def piece_of(array, k):
    me = lax.axis_index("zq")
    sent = lax.dynamic_slice_in_dim(array, ((me + k) & 3) * QUARTER, QUARTER, 0)
    return hop(sent, "zq", k), ((me + 4 - k) & 3) * QUARTER


def pair_of(arrays, k):
    me = lax.axis_index("zq")
    at = ((me + k) & 3) * QUARTER
    sent = [lax.dynamic_slice_in_dim(array, at, QUARTER, 0) for array in arrays]
    return hop(jnp.concatenate(sent, axis=0), "zq", k), ((me + 4 - k) & 3) * QUARTER


def placed(array, pieces):
    for piece, at in pieces:
        array = lax.dynamic_update_slice_in_dim(array, piece, at, 0)
    return array


def pack_kernel(wide_one, narrow_one, wide_two, narrow_two, out):
    for at, (wide, narrow) in enumerate(((wide_one, narrow_one), (wide_two, narrow_two))):
        for copy in range(8):
            for tap in range(3):
                out[copy, :, (4 * at + tap) * COLS : (4 * at + tap + 1) * COLS] = wide[tap]
            out[copy, :, (4 * at + 3) * COLS : (4 * at + 4) * COLS] = narrow[...]


def unpack_kernel(own, got, wide_one, narrow_one, wide_two, narrow_two):
    total = (own[0].astype(F32) + got[0].astype(F32)).astype(BF)
    for at, (wide, narrow) in enumerate(((wide_one, narrow_one), (wide_two, narrow_two))):
        for tap in range(3):
            wide[tap] = total[:, (4 * at + tap) * COLS : (4 * at + tap + 1) * COLS]
        narrow[...] = total[:, (4 * at + 3) * COLS : (4 * at + 4) * COLS]


def body(inputs, upstream, wide_one, narrow_one, wide_two, narrow_two):
    own = pl.pallas_call(
        pack_kernel, out_shape=jax.ShapeDtypeStruct((8, 3, 8 * COLS), BF), name="pack_rows"
    )(wide_one, narrow_one, wide_two, narrow_two)
    rows_z = lax.all_to_all(own, RING_Z, 0, 0, tiled=True).reshape(24, 8 * COLS)
    raw = inputs[0]
    next_x, last_x = piece_of(raw, 1), piece_of(raw, 3)
    rows_z = after(rows_z, next_x[0], last_x[0])
    far_x = piece_of(after(raw, rows_z), 2)
    rows_one = collect_pairs(rows_z[:, : 4 * COLS], "x")
    rows_two = collect_pairs(rows_z[:, 4 * COLS :], RING_Y)
    rows_one = collect(after(rows_one, far_x[0]), RING_Y)
    far_two, next_two = hop(rows_two, "x", 2), hop(rows_two, "x", 1)
    rows_one = after(rows_one, far_two, next_two)
    x = placed(raw, (next_x, last_x, far_x))
    raw = after(upstream[0], far_x[0])
    next_g = piece_of(raw, 1)
    act1, slope_x = gelu_parts(x.astype(F32))
    act1 = act1.astype(BF)
    lower1 = jnp.concatenate([along(act1[3 * QUARTER :], 1), act1[: 3 * QUARTER]], axis=0)
    upper1 = jnp.concatenate([act1[QUARTER:], along(act1[:QUARTER], -1)], axis=0)

    channels = lax.iota(jnp.int32, ROWS)

    def unmixed(rows, x_first):
        return dot_plain((slot_owner(-1, x_first)[None, :] == channels[:, None]).astype(BF), rows).astype(BF)

    mix_one = (slot_owner(1, False)[:, None] == channels[None, :]).astype(BF)
    mix_two = (slot_owner(1, True)[:, None] == channels[None, :]).astype(BF)

    k1 = unmixed(collect_pairs(rows_one, "core"), False)
    last_two = hop(after(rows_two, k1), "x", 3)
    rows_two = jnp.concatenate([rows_two, next_two, far_two, last_two], axis=0)
    last_g = piece_of(after(raw, k1), 3)

    def tap(k, i):
        return k[:, i * COLS : (i + 1) * COLS]

    pre1 = (
        dot_plain(act1, tap(k1, 1))
        + dot_plain(lower1, tap(k1, 0))
        + dot_plain(upper1, tap(k1, 2))
    )
    inner1, slope1 = gelu_parts(pre1)
    inner1 = inner1.astype(BF)
    middle = (x.astype(F32) + dot_back(inner1, tap(k1, 3))).astype(BF)
    k2 = unmixed(collect_pairs(after(rows_two, middle), "core"), True)

    half = 2 * QUARTER
    act2, slope_m = gelu_parts(middle.astype(F32))
    act2 = act2.astype(BF)
    first, third = dot_plain(act2, tap(k2, 0)), dot_plain(act2, tap(k2, 2))
    to_later = along(first[half:].astype(BF), 1).astype(F32)
    to_earlier = along(third[:half].astype(BF), -1).astype(F32)
    far_g = piece_of(after(raw, first), 2)
    pre2 = (
        dot_plain(act2, tap(k2, 1))
        + jnp.concatenate([to_later, first[:half]], axis=0)
        + jnp.concatenate([third[half:], to_earlier], axis=0)
    )
    inner2, slope2 = gelu_parts(pre2)
    inner2 = inner2.astype(BF)
    g = placed(raw, (next_g, last_g, far_g))

    dpre2 = (dot_plain(g, tap(k2, 3)) * slope2).astype(BF)
    from_later, from_earlier = along(dpre2[:half], -1), along(dpre2[half:], 1)
    trio2 = jnp.concatenate(
        [
            jnp.concatenate([dpre2[half:], from_later], axis=0),
            dpre2,
            jnp.concatenate([from_earlier, dpre2[:half]], axis=0),
        ],
        axis=1,
    )
    grads2 = jnp.concatenate([dot_rows(act2, trio2).astype(BF), dot_rows(g, inner2).astype(BF)], axis=1)
    sent2 = dot_plain(mix_two[COLS:], grads2).astype(BF)
    got2 = swap(sent2, "core", 1)
    trio2 = after(trio2, sent2)
    dact2 = dot_back(trio2, k2[:, : 3 * COLS])
    middle_grad = (g.astype(F32) + dact2 * slope_m).astype(BF)

    dpre1 = (dot_plain(middle_grad, tap(k1, 3)) * slope1).astype(BF)
    dpre1 = after(dpre1, got2)
    part2 = total_of(dot_plain(mix_two[:COLS], grads2).astype(BF), got2)
    near2, far2 = spread_half(part2, "x", 3)
    trio1 = jnp.concatenate(
        [
            jnp.concatenate([dpre1[QUARTER:], along(dpre1[:QUARTER], -1)], axis=0),
            dpre1,
            jnp.concatenate([along(dpre1[3 * QUARTER :], 1), dpre1[: 3 * QUARTER]], axis=0),
        ],
        axis=1,
    )
    dpre1 = after(dpre1, part2)
    grads1 = jnp.concatenate(
        [
            dot_rows(lower1, dpre1).astype(BF),
            dot_rows(act1, dpre1).astype(BF),
            dot_rows(upper1, dpre1).astype(BF),
            dot_rows(middle_grad, inner1).astype(BF),
        ],
        axis=1,
    )
    sent1 = dot_plain(mix_one[COLS:], grads1).astype(BF)
    got1 = swap(sent1, "core", 1)
    kept1 = dot_plain(mix_one[:COLS], after(grads1, sent1)).astype(BF)
    dact1 = dot_back(after(trio1, sent1), k1[:, : 3 * COLS])
    cotangent = (middle_grad.astype(F32) + dact1 * slope_x).astype(BF)
    result = middle.astype(F32) + dot_back(after(inner2, sent1), tap(k2, 3))
    result = result.astype(BF)
    part1 = total_of(kept1, got1)
    pieces = [pair_of((after(cotangent, part1), after(result, part1)), 2)]
    part1 = spread(part1, RING_Y)
    part2 = total_of(*spread_half(total_of(near2, after(far2, part1[1])), "x", 1))
    ready = after(cotangent, part1[1]), after(result, part1[1])
    pieces += [pair_of(ready, k) for k in (1, 3)]
    cotangent = placed(cotangent, [(pair[:QUARTER], at) for pair, at in pieces])
    result = placed(result, [(pair[QUARTER:], at) for pair, at in pieces])

    part1 = spread_pairs(total_of(*part1), "x")
    part2 = spread_pairs(part2, RING_Y)
    both = jnp.concatenate([part1, part2], axis=1).reshape(8, 3, 8 * COLS)
    both = spread_pairs(both, "zq")
    wide = jax.ShapeDtypeStruct((3, 3, COLS), BF)
    narrow = jax.ShapeDtypeStruct((3, COLS), BF)
    grads = pl.pallas_call(
        unpack_kernel, out_shape=(wide, narrow, wide, narrow), name="sum_rows"
    )(both[:1], swap(both[1:], "zp", 1))
    return (result[None], cotangent[None], *grads)


def solution(mesh):
    names = ("yl", "x", "zq", "zp", "yh", "core")
    fine = Mesh(mesh.devices.reshape(2, 4, 4, 2, 2, 2), names)
    seq, batch = names[:4], names[4:]
    specs = (
        P(batch, seq, None),
        P(batch, seq, None),
        P(None, seq + batch, None),
        P(seq + batch, None),
        P(None, seq + batch, None),
        P(seq + batch, None),
    )
    return jax.shard_map(body, mesh=fine, in_specs=specs, out_specs=specs, check_vma=False)
```

```python
import jax
import jax.numpy as jnp
from jax import lax
from jax.experimental import pallas as pl
from jax.experimental.pallas import tpu as pltpu
from jax.sharding import Mesh, PartitionSpec as P

BF = jnp.bfloat16
F32 = jnp.float32
LINE = ("yl", "x")
RING_Y = ("yl", "yh")
RING_Z = ("zq", "zp")
COLS = 384
ROWS = 768
QUARTER = 128


def gelu_parts(v):
    cdf = 0.5 * (1.0 + lax.erf(v * 0.7071067811865476))
    slope = cdf + v * jnp.exp(-0.5 * v * v) * 0.3989422804014327
    return v * cdf, slope


def dot_plain(left, right):
    return jnp.dot(left, right, preferred_element_type=F32)


def dot_rows(left, right):
    return lax.dot_general(left, right, (((0,), (0,)), ((), ())), preferred_element_type=F32)


def dot_back(left, right):
    return lax.dot_general(left, right, (((1,), (1,)), ((), ())), preferred_element_type=F32)


def after(value, *others):
    return lax.optimization_barrier((value, *others))[0]


def along(array, by):
    count = lax.axis_size(LINE)
    got = lax.ppermute(array, LINE, [(i, (i + by) % count) for i in range(count)])
    end = 0 if by > 0 else count - 1
    return jnp.where(lax.axis_index(LINE) == end, jnp.zeros_like(got), got)


def permuted(array, axis, target):
    count = lax.axis_size(axis)
    place = (lambda y: y % 2 * 2 + y // 2) if axis == RING_Y else (lambda i: i)
    return lax.ppermute(array, axis, [(place(i), place(target(i) % count)) for i in range(count)])


def hop(array, axis, by):
    return permuted(array, axis, lambda i: i + by)


def swap(array, axis, bits):
    return permuted(array, axis, lambda i: i ^ bits)


def collect(rows, axis):
    count = lax.axis_size(axis)
    return jnp.concatenate([rows] + [hop(rows, axis, k) for k in range(1, count)], axis=0)


def collect_pairs(rows, axis):
    rows = jnp.concatenate([rows, swap(rows, axis, 1)], axis=0)
    if lax.axis_size(axis) == 4:
        rows = jnp.concatenate([rows, swap(rows, axis, 3)], axis=0)
    return rows


def total_of(own, *others):
    total = own.astype(F32)
    for other in others:
        total = total + other.astype(F32)
    return total.astype(BF)


def spread(rows, axis):
    count = lax.axis_size(axis)
    size = rows.shape[0] // count
    return [rows[:size]] + [hop(rows[k * size : (k + 1) * size], axis, k) for k in range(1, count)]


def spread_half(rows, axis, bits):
    half = rows.shape[0] // 2
    return rows[:half], swap(rows[half:], axis, bits)


def spread_pairs(rows, axis):
    return total_of(*spread_half(total_of(*spread_half(rows, axis, 3)), axis, 1))


def slot_owner(gather, y_pairs):
    slot = lax.iota(jnp.int32, ROWS)
    k = lax.div(slot, jnp.int32(3))
    row = slot - 3 * k
    kp, kq, kx, ky, kc = k & 1, (k >> 1) & 3, (k >> 3) & 3, (k >> 5) & 3, k >> 7
    zp, zq = kp, kq
    if not gather:
        zp, zq = lax.axis_index("zp") ^ kp, lax.axis_index("zq") ^ (kq ^ (kq >> 1))
    x = lax.axis_index("x") ^ (kx ^ (kx >> 1))
    y = lax.axis_index("yh") * 2 + lax.axis_index("yl")
    if y_pairs:
        y = y ^ (ky ^ (ky >> 1))
    else:
        y = (y - ky + 4) & 3 if gather else (y + ky) & 3
    c = lax.axis_index("core") ^ kc
    yh, yl = y >> 1, y & 1
    return ((((yl * 4 + x) * 8 + zq * 2 + zp) * 2 + yh) * 2 + c) * 3 + row


def exchange(array):
    swapped = lax.all_to_all(array.reshape(4, QUARTER, ROWS), "zq", 0, 0, tiled=True)
    return swapped.reshape(4 * QUARTER, ROWS)


def pair_of(arrays, k):
    me = lax.axis_index("zq")
    at = ((me + k) & 3) * QUARTER
    sent = [lax.dynamic_slice_in_dim(array, at, QUARTER, 0) for array in arrays]
    return hop(jnp.concatenate(sent, axis=0), "zq", k), ((me + 4 - k) & 3) * QUARTER


def placed(array, pieces):
    for piece, at in pieces:
        array = lax.dynamic_update_slice_in_dim(array, piece, at, 0)
    return array


def pack_kernel(wide_one, narrow_one, wide_two, narrow_two, out):
    for at, (wide, narrow) in enumerate(((wide_one, narrow_one), (wide_two, narrow_two))):
        for copy in range(8):
            for tap in range(3):
                out[copy, :, (4 * at + tap) * COLS : (4 * at + tap + 1) * COLS] = wide[tap]
            out[copy, :, (4 * at + 3) * COLS : (4 * at + 4) * COLS] = narrow[...]


def unpack_kernel(own, got, wide_one, narrow_one, wide_two, narrow_two):
    total = (own[0].astype(F32) + got[0].astype(F32)).astype(BF)
    for at, (wide, narrow) in enumerate(((wide_one, narrow_one), (wide_two, narrow_two))):
        for tap in range(3):
            wide[tap] = total[:, (4 * at + tap) * COLS : (4 * at + tap + 1) * COLS]
        narrow[...] = total[:, (4 * at + 3) * COLS : (4 * at + 4) * COLS]


def body(inputs, upstream, wide_one, narrow_one, wide_two, narrow_two):
    own = pl.pallas_call(
        pack_kernel, out_shape=jax.ShapeDtypeStruct((8, 3, 8 * COLS), BF), name="pack_rows"
    )(wide_one, narrow_one, wide_two, narrow_two)
    rows_z = lax.all_to_all(own, RING_Z, 0, 0, tiled=True).reshape(24, 8 * COLS)
    x = exchange(after(inputs[0], rows_z))
    rows_x = collect_pairs(rows_z, "x")
    g = exchange(after(upstream[0], x))
    act1, slope_x = gelu_parts(x.astype(F32))
    act1 = act1.astype(BF)
    below, above = along(act1[3 * QUARTER :], 1), along(act1[:QUARTER], -1)
    lower1 = jnp.concatenate([below, act1[: 3 * QUARTER]], axis=0)
    upper1 = jnp.concatenate([act1[QUARTER:], above], axis=0)

    channels = lax.iota(jnp.int32, ROWS)

    def unmixed(rows):
        return dot_plain((slot_owner(True, False)[None, :] == channels[:, None]).astype(BF), rows).astype(BF)

    mix_one = (slot_owner(False, False)[:, None] == channels[None, :]).astype(BF)
    mix_two = (slot_owner(False, True)[:, None] == channels[None, :]).astype(BF)

    rows = collect_pairs(after(collect(rows_x, RING_Y), below, above), "core")
    k1, k2 = unmixed(rows[:, : 4 * COLS]), unmixed(rows[:, 4 * COLS :])

    def tap(k, i):
        return k[:, i * COLS : (i + 1) * COLS]

    pre1 = (
        dot_plain(act1, tap(k1, 1))
        + dot_plain(lower1, tap(k1, 0))
        + dot_plain(upper1, tap(k1, 2))
    )
    inner1, slope1 = gelu_parts(pre1)
    inner1 = inner1.astype(BF)
    middle = (x.astype(F32) + dot_back(inner1, tap(k1, 3))).astype(BF)

    half = 2 * QUARTER
    act2, slope_m = gelu_parts(middle.astype(F32))
    act2 = act2.astype(BF)
    first, third = dot_plain(act2, tap(k2, 0)), dot_plain(act2, tap(k2, 2))
    to_later = along(first[half:].astype(BF), 1).astype(F32)
    to_earlier = along(third[:half].astype(BF), -1).astype(F32)
    pre2 = (
        dot_plain(act2, tap(k2, 1))
        + jnp.concatenate([to_later, first[:half]], axis=0)
        + jnp.concatenate([third[half:], to_earlier], axis=0)
    )
    inner2, slope2 = gelu_parts(pre2)
    inner2 = inner2.astype(BF)

    dpre2 = (dot_plain(g, tap(k2, 3)) * slope2).astype(BF)
    from_later, from_earlier = along(dpre2[:half], -1), along(dpre2[half:], 1)
    trio2 = jnp.concatenate(
        [
            jnp.concatenate([dpre2[half:], from_later], axis=0),
            dpre2,
            jnp.concatenate([from_earlier, dpre2[:half]], axis=0),
        ],
        axis=1,
    )
    grads2 = jnp.concatenate([dot_rows(act2, trio2).astype(BF), dot_rows(g, inner2).astype(BF)], axis=1)
    sent2 = dot_plain(mix_two[COLS:], grads2).astype(BF)
    got2 = swap(sent2, "core", 1)
    trio2 = after(trio2, sent2)
    dact2 = dot_back(trio2, k2[:, : 3 * COLS])
    middle_grad = (g.astype(F32) + dact2 * slope_m).astype(BF)

    dpre1 = (dot_plain(middle_grad, tap(k1, 3)) * slope1).astype(BF)
    dpre1 = after(dpre1, got2)
    part2 = total_of(dot_plain(mix_two[:COLS], grads2).astype(BF), got2)
    near2, far2 = spread_half(part2, RING_Y, 3)
    trio1 = jnp.concatenate(
        [
            jnp.concatenate([dpre1[QUARTER:], along(dpre1[:QUARTER], -1)], axis=0),
            dpre1,
            jnp.concatenate([along(dpre1[3 * QUARTER :], 1), dpre1[: 3 * QUARTER]], axis=0),
        ],
        axis=1,
    )
    dpre1 = after(dpre1, part2)
    grads1 = jnp.concatenate(
        [
            dot_rows(lower1, dpre1).astype(BF),
            dot_rows(act1, dpre1).astype(BF),
            dot_rows(upper1, dpre1).astype(BF),
            dot_rows(middle_grad, inner1).astype(BF),
        ],
        axis=1,
    )
    sent1 = dot_plain(mix_one[COLS:], grads1).astype(BF)
    got1 = swap(sent1, "core", 1)
    kept1 = dot_plain(mix_one[:COLS], after(grads1, sent1)).astype(BF)
    dact1 = dot_back(after(trio1, sent1), k1[:, : 3 * COLS])
    cotangent = (middle_grad.astype(F32) + dact1 * slope_x).astype(BF)
    result = middle.astype(F32) + dot_back(after(inner2, sent1), tap(k2, 3))
    result = result.astype(BF)
    part1 = total_of(kept1, got1)
    pieces = [pair_of((after(cotangent, part1), after(result, part1)), 2)]
    part1 = spread(part1, RING_Y)
    part2 = total_of(*spread_half(total_of(near2, after(far2, part1[1])), RING_Y, 1))
    ready = after(cotangent, part1[1]), after(result, part1[1])
    pieces += [pair_of(ready, k) for k in (1, 3)]
    cotangent = placed(cotangent, [(pair[:QUARTER], at) for pair, at in pieces])
    result = placed(result, [(pair[QUARTER:], at) for pair, at in pieces])

    both = spread_pairs(jnp.concatenate([total_of(*part1), part2], axis=1), "x")
    both = spread_pairs(both.reshape(8, 3, 8 * COLS), "zq")
    wide = jax.ShapeDtypeStruct((3, 3, COLS), BF)
    narrow = jax.ShapeDtypeStruct((3, COLS), BF)
    grads = pl.pallas_call(
        unpack_kernel, out_shape=(wide, narrow, wide, narrow), name="sum_rows"
    )(both[:1], swap(both[1:], "zp", 1))
    return (result[None], cotangent[None], *grads)


def solution(mesh):
    names = ("yl", "x", "zq", "zp", "yh", "core")
    fine = Mesh(mesh.devices.reshape(2, 4, 4, 2, 2, 2), names)
    seq, batch = names[:4], names[4:]
    specs = (
        P(batch, seq, None),
        P(batch, seq, None),
        P(None, seq + batch, None),
        P(seq + batch, None),
        P(None, seq + batch, None),
        P(seq + batch, None),
    )
    return jax.shard_map(body, mesh=fine, in_specs=specs, out_specs=specs, check_vma=False)
```

```python
import jax
import jax.numpy as jnp
from jax import lax
from jax.experimental import pallas as pl
from jax.experimental.pallas import tpu as pltpu
from jax.sharding import Mesh, PartitionSpec as P

BF = jnp.bfloat16
F32 = jnp.float32
LINE = ("yl", "x")
RING_Y = ("yl", "yh")
RING_Z = ("zq", "zp")
COLS = 384
ROWS = 768
QUARTER = 128


def gelu_parts(v):
    cdf = 0.5 * (1.0 + lax.erf(v * 0.7071067811865476))
    slope = cdf + v * jnp.exp(-0.5 * v * v) * 0.3989422804014327
    return v * cdf, slope


def dot_plain(left, right):
    return jnp.dot(left, right, preferred_element_type=F32)


def dot_rows(left, right):
    return lax.dot_general(left, right, (((0,), (0,)), ((), ())), preferred_element_type=F32)


def dot_back(left, right):
    return lax.dot_general(left, right, (((1,), (1,)), ((), ())), preferred_element_type=F32)


def after(value, *others):
    return lax.optimization_barrier((value, *others))[0]


def along(array, by):
    count = lax.axis_size(LINE)
    got = lax.ppermute(array, LINE, [(i, (i + by) % count) for i in range(count)])
    end = 0 if by > 0 else count - 1
    return jnp.where(lax.axis_index(LINE) == end, jnp.zeros_like(got), got)


def permuted(array, axis, target):
    count = lax.axis_size(axis)
    place = (lambda y: y % 2 * 2 + y // 2) if axis == RING_Y else (lambda i: i)
    return lax.ppermute(array, axis, [(place(i), place(target(i) % count)) for i in range(count)])


def hop(array, axis, by):
    return permuted(array, axis, lambda i: i + by)


def swap(array, axis, bits):
    return permuted(array, axis, lambda i: i ^ bits)


def collect(rows, axis):
    count = lax.axis_size(axis)
    return jnp.concatenate([rows] + [hop(rows, axis, k) for k in range(1, count)], axis=0)


def collect_pairs(rows, axis):
    rows = jnp.concatenate([rows, swap(rows, axis, 1)], axis=0)
    if lax.axis_size(axis) == 4:
        rows = jnp.concatenate([rows, swap(rows, axis, 3)], axis=0)
    return rows


def total_of(own, *others):
    total = own.astype(F32)
    for other in others:
        total = total + other.astype(F32)
    return total.astype(BF)


def spread(rows, axis):
    count = lax.axis_size(axis)
    size = rows.shape[0] // count
    return [rows[:size]] + [hop(rows[k * size : (k + 1) * size], axis, k) for k in range(1, count)]


def spread_half(rows, axis, bits):
    half = rows.shape[0] // 2
    return rows[:half], swap(rows[half:], axis, bits)


def spread_pairs(rows, axis):
    return total_of(*spread_half(total_of(*spread_half(rows, axis, 3)), axis, 1))


def slot_owner(sign, x_first):
    slot = lax.iota(jnp.int32, ROWS)
    k = lax.div(slot, jnp.int32(3))
    row = slot - 3 * k
    kp, kq, k_in, k_out, kc = k & 1, (k >> 1) & 3, (k >> 3) & 3, (k >> 5) & 3, k >> 7
    zp, zq = kp, kq
    if sign > 0:
        zp, zq = lax.axis_index("zp") ^ kp, lax.axis_index("zq") ^ (kq ^ (kq >> 1))
    x, y = lax.axis_index("x"), lax.axis_index("yh") * 2 + lax.axis_index("yl")
    if x_first:
        y = y ^ (k_in ^ (k_in >> 1))
        x = x ^ (k_out ^ (k_out >> 1)) if sign > 0 else (x - k_out + 4) & 3
    else:
        x, y = x ^ (k_in ^ (k_in >> 1)), (y + sign * k_out + 4) & 3
    c = lax.axis_index("core") ^ kc
    yh, yl = y >> 1, y & 1
    return ((((yl * 4 + x) * 8 + zq * 2 + zp) * 2 + yh) * 2 + c) * 3 + row


def exchange(array):
    swapped = lax.all_to_all(array.reshape(4, QUARTER, ROWS), "zq", 0, 0, tiled=True)
    return swapped.reshape(4 * QUARTER, ROWS)


def pair_of(arrays, k):
    me = lax.axis_index("zq")
    at = ((me + k) & 3) * QUARTER
    sent = [lax.dynamic_slice_in_dim(array, at, QUARTER, 0) for array in arrays]
    return hop(jnp.concatenate(sent, axis=0), "zq", k), ((me + 4 - k) & 3) * QUARTER


def placed(array, pieces):
    for piece, at in pieces:
        array = lax.dynamic_update_slice_in_dim(array, piece, at, 0)
    return array


def pack_kernel(wide_one, narrow_one, wide_two, narrow_two, out):
    for at, (wide, narrow) in enumerate(((wide_one, narrow_one), (wide_two, narrow_two))):
        for copy in range(8):
            for tap in range(3):
                out[copy, :, (4 * at + tap) * COLS : (4 * at + tap + 1) * COLS] = wide[tap]
            out[copy, :, (4 * at + 3) * COLS : (4 * at + 4) * COLS] = narrow[...]


def unpack_kernel(own, got, wide_one, narrow_one, wide_two, narrow_two):
    total = (own[0].astype(F32) + got[0].astype(F32)).astype(BF)
    for at, (wide, narrow) in enumerate(((wide_one, narrow_one), (wide_two, narrow_two))):
        for tap in range(3):
            wide[tap] = total[:, (4 * at + tap) * COLS : (4 * at + tap + 1) * COLS]
        narrow[...] = total[:, (4 * at + 3) * COLS : (4 * at + 4) * COLS]


def body(inputs, upstream, wide_one, narrow_one, wide_two, narrow_two):
    own = pl.pallas_call(
        pack_kernel, out_shape=jax.ShapeDtypeStruct((8, 3, 8 * COLS), BF), name="pack_rows"
    )(wide_one, narrow_one, wide_two, narrow_two)
    rows_z = lax.all_to_all(own, RING_Z, 0, 0, tiled=True).reshape(24, 8 * COLS)
    x = exchange(after(inputs[0], rows_z))
    rows_one = collect_pairs(rows_z[:, : 4 * COLS], "x")
    rows_two = collect_pairs(rows_z[:, 4 * COLS :], RING_Y)
    rows_one = collect(rows_one, RING_Y)
    far_two, next_two = hop(rows_two, "x", 2), hop(rows_two, "x", 1)
    rows_one = after(rows_one, far_two, next_two)
    g = exchange(after(upstream[0], x))
    act1, slope_x = gelu_parts(x.astype(F32))
    act1 = act1.astype(BF)
    lower1 = jnp.concatenate([along(act1[3 * QUARTER :], 1), act1[: 3 * QUARTER]], axis=0)
    upper1 = jnp.concatenate([act1[QUARTER:], along(act1[:QUARTER], -1)], axis=0)

    channels = lax.iota(jnp.int32, ROWS)

    def unmixed(rows, x_first):
        return dot_plain((slot_owner(-1, x_first)[None, :] == channels[:, None]).astype(BF), rows).astype(BF)

    mix_one = (slot_owner(1, False)[:, None] == channels[None, :]).astype(BF)
    mix_two = (slot_owner(1, True)[:, None] == channels[None, :]).astype(BF)

    k1 = unmixed(collect_pairs(rows_one, "core"), False)
    last_two = hop(after(rows_two, k1), "x", 3)
    rows_two = jnp.concatenate([rows_two, next_two, far_two, last_two], axis=0)

    def tap(k, i):
        return k[:, i * COLS : (i + 1) * COLS]

    pre1 = (
        dot_plain(act1, tap(k1, 1))
        + dot_plain(lower1, tap(k1, 0))
        + dot_plain(upper1, tap(k1, 2))
    )
    inner1, slope1 = gelu_parts(pre1)
    inner1 = inner1.astype(BF)
    middle = (x.astype(F32) + dot_back(inner1, tap(k1, 3))).astype(BF)
    k2 = unmixed(collect_pairs(after(rows_two, middle), "core"), True)

    half = 2 * QUARTER
    act2, slope_m = gelu_parts(middle.astype(F32))
    act2 = act2.astype(BF)
    first, third = dot_plain(act2, tap(k2, 0)), dot_plain(act2, tap(k2, 2))
    to_later = along(first[half:].astype(BF), 1).astype(F32)
    to_earlier = along(third[:half].astype(BF), -1).astype(F32)
    pre2 = (
        dot_plain(act2, tap(k2, 1))
        + jnp.concatenate([to_later, first[:half]], axis=0)
        + jnp.concatenate([third[half:], to_earlier], axis=0)
    )
    inner2, slope2 = gelu_parts(pre2)
    inner2 = inner2.astype(BF)

    dpre2 = (dot_plain(g, tap(k2, 3)) * slope2).astype(BF)
    from_later, from_earlier = along(dpre2[:half], -1), along(dpre2[half:], 1)
    trio2 = jnp.concatenate(
        [
            jnp.concatenate([dpre2[half:], from_later], axis=0),
            dpre2,
            jnp.concatenate([from_earlier, dpre2[:half]], axis=0),
        ],
        axis=1,
    )
    grads2 = jnp.concatenate([dot_rows(act2, trio2).astype(BF), dot_rows(g, inner2).astype(BF)], axis=1)
    sent2 = dot_plain(mix_two[COLS:], grads2).astype(BF)
    got2 = swap(sent2, "core", 1)
    trio2 = after(trio2, sent2)
    dact2 = dot_back(trio2, k2[:, : 3 * COLS])
    middle_grad = (g.astype(F32) + dact2 * slope_m).astype(BF)

    dpre1 = (dot_plain(middle_grad, tap(k1, 3)) * slope1).astype(BF)
    dpre1 = after(dpre1, got2)
    part2 = total_of(dot_plain(mix_two[:COLS], grads2).astype(BF), got2)
    near2, far2 = spread_half(part2, "x", 3)
    trio1 = jnp.concatenate(
        [
            jnp.concatenate([dpre1[QUARTER:], along(dpre1[:QUARTER], -1)], axis=0),
            dpre1,
            jnp.concatenate([along(dpre1[3 * QUARTER :], 1), dpre1[: 3 * QUARTER]], axis=0),
        ],
        axis=1,
    )
    dpre1 = after(dpre1, part2)
    grads1 = jnp.concatenate(
        [
            dot_rows(lower1, dpre1).astype(BF),
            dot_rows(act1, dpre1).astype(BF),
            dot_rows(upper1, dpre1).astype(BF),
            dot_rows(middle_grad, inner1).astype(BF),
        ],
        axis=1,
    )
    sent1 = dot_plain(mix_one[COLS:], grads1).astype(BF)
    got1 = swap(sent1, "core", 1)
    kept1 = dot_plain(mix_one[:COLS], after(grads1, sent1)).astype(BF)
    dact1 = dot_back(after(trio1, sent1), k1[:, : 3 * COLS])
    cotangent = (middle_grad.astype(F32) + dact1 * slope_x).astype(BF)
    result = middle.astype(F32) + dot_back(after(inner2, sent1), tap(k2, 3))
    result = result.astype(BF)
    part1 = total_of(kept1, got1)
    pieces = [pair_of((after(cotangent, part1), after(result, part1)), 2)]
    part1 = spread(part1, RING_Y)
    part2 = total_of(*spread_half(total_of(near2, after(far2, part1[1])), "x", 1))
    ready = after(cotangent, part1[1]), after(result, part1[1])
    pieces += [pair_of(ready, k) for k in (1, 3)]
    cotangent = placed(cotangent, [(pair[:QUARTER], at) for pair, at in pieces])
    result = placed(result, [(pair[QUARTER:], at) for pair, at in pieces])

    part1 = spread_pairs(total_of(*part1), "x")
    part2 = spread_pairs(part2, RING_Y)
    both = jnp.concatenate([part1, part2], axis=1).reshape(8, 3, 8 * COLS)
    both = spread_pairs(both, "zq")
    wide = jax.ShapeDtypeStruct((3, 3, COLS), BF)
    narrow = jax.ShapeDtypeStruct((3, COLS), BF)
    grads = pl.pallas_call(
        unpack_kernel, out_shape=(wide, narrow, wide, narrow), name="sum_rows"
    )(both[:1], swap(both[1:], "zp", 1))
    return (result[None], cotangent[None], *grads)


def solution(mesh):
    names = ("yl", "x", "zq", "zp", "yh", "core")
    fine = Mesh(mesh.devices.reshape(2, 4, 4, 2, 2, 2), names)
    seq, batch = names[:4], names[4:]
    specs = (
        P(batch, seq, None),
        P(batch, seq, None),
        P(None, seq + batch, None),
        P(seq + batch, None),
        P(None, seq + batch, None),
        P(seq + batch, None),
    )
    return jax.shard_map(body, mesh=fine, in_specs=specs, out_specs=specs, check_vma=False)
```

```python
import jax
import jax.numpy as jnp
from jax import lax
from jax.experimental import pallas as pl
from jax.experimental.pallas import tpu as pltpu
from jax.sharding import Mesh, PartitionSpec as P

BF = jnp.bfloat16
F32 = jnp.float32
LINE = ("yl", "x")
RING_Y = ("yl", "yh")
RING_Z = ("zq", "zp")
COLS = 384
ROWS = 768
QUARTER = 128


def gelu_parts(v):
    cdf = 0.5 * (1.0 + lax.erf(v * 0.7071067811865476))
    slope = cdf + v * jnp.exp(-0.5 * v * v) * 0.3989422804014327
    return v * cdf, slope


def dot_plain(left, right):
    return jnp.dot(left, right, preferred_element_type=F32)


def dot_rows(left, right):
    return lax.dot_general(left, right, (((0,), (0,)), ((), ())), preferred_element_type=F32)


def dot_back(left, right):
    return lax.dot_general(left, right, (((1,), (1,)), ((), ())), preferred_element_type=F32)


def after(value, *others):
    return lax.optimization_barrier((value, *others))[0]


def along(array, by):
    count = lax.axis_size(LINE)
    got = lax.ppermute(array, LINE, [(i, (i + by) % count) for i in range(count)])
    end = 0 if by > 0 else count - 1
    return jnp.where(lax.axis_index(LINE) == end, jnp.zeros_like(got), got)


def permuted(array, axis, target):
    count = lax.axis_size(axis)
    place = (lambda y: y % 2 * 2 + y // 2) if axis == RING_Y else (lambda i: i)
    return lax.ppermute(array, axis, [(place(i), place(target(i) % count)) for i in range(count)])


def hop(array, axis, by):
    return permuted(array, axis, lambda i: i + by)


def swap(array, axis, bits):
    return permuted(array, axis, lambda i: i ^ bits)


def collect(rows, axis):
    count = lax.axis_size(axis)
    return jnp.concatenate([rows] + [hop(rows, axis, k) for k in range(1, count)], axis=0)


def collect_pairs(rows, axis):
    rows = jnp.concatenate([rows, swap(rows, axis, 1)], axis=0)
    if lax.axis_size(axis) == 4:
        rows = jnp.concatenate([rows, swap(rows, axis, 3)], axis=0)
    return rows


def total_of(own, *others):
    total = own.astype(F32)
    for other in others:
        total = total + other.astype(F32)
    return total.astype(BF)


def spread(rows, axis):
    count = lax.axis_size(axis)
    size = rows.shape[0] // count
    return [rows[:size]] + [hop(rows[k * size : (k + 1) * size], axis, k) for k in range(1, count)]


def spread_half(rows, axis, bits):
    half = rows.shape[0] // 2
    return rows[:half], swap(rows[half:], axis, bits)


def spread_pairs(rows, axis):
    return total_of(*spread_half(total_of(*spread_half(rows, axis, 3)), axis, 1))


def slot_owner(sign, x_first):
    slot = lax.iota(jnp.int32, ROWS)
    k = lax.div(slot, jnp.int32(3))
    row = slot - 3 * k
    kp, kq, k_in, k_out, kc = k & 1, (k >> 1) & 3, (k >> 3) & 3, (k >> 5) & 3, k >> 7
    zp, zq = kp, kq
    if sign > 0:
        zp, zq = lax.axis_index("zp") ^ kp, lax.axis_index("zq") ^ (kq ^ (kq >> 1))
    x, y = lax.axis_index("x"), lax.axis_index("yh") * 2 + lax.axis_index("yl")
    if x_first:
        y = y ^ (k_in ^ (k_in >> 1))
        x = x ^ (k_out ^ (k_out >> 1)) if sign > 0 else (x - k_out + 4) & 3
    else:
        x, y = x ^ (k_in ^ (k_in >> 1)), (y + sign * k_out + 4) & 3
    c = lax.axis_index("core") ^ kc
    yh, yl = y >> 1, y & 1
    return ((((yl * 4 + x) * 8 + zq * 2 + zp) * 2 + yh) * 2 + c) * 3 + row


def exchange(array):
    swapped = lax.all_to_all(array.reshape(4, QUARTER, ROWS), "zq", 0, 0, tiled=True)
    return swapped.reshape(4 * QUARTER, ROWS)


def pair_of(arrays, k):
    me = lax.axis_index("zq")
    at = ((me + k) & 3) * QUARTER
    sent = [lax.dynamic_slice_in_dim(array, at, QUARTER, 0) for array in arrays]
    return hop(jnp.concatenate(sent, axis=0), "zq", k), ((me + 4 - k) & 3) * QUARTER


def placed(array, pieces):
    for piece, at in pieces:
        array = lax.dynamic_update_slice_in_dim(array, piece, at, 0)
    return array


def pack_kernel(wide_one, narrow_one, wide_two, narrow_two, out):
    for at, (wide, narrow) in enumerate(((wide_one, narrow_one), (wide_two, narrow_two))):
        for copy in range(8):
            for tap in range(3):
                out[copy, :, (4 * at + tap) * COLS : (4 * at + tap + 1) * COLS] = wide[tap]
            out[copy, :, (4 * at + 3) * COLS : (4 * at + 4) * COLS] = narrow[...]


def unpack_kernel(own, got, wide_one, narrow_one, wide_two, narrow_two):
    total = (own[0].astype(F32) + got[0].astype(F32)).astype(BF)
    for at, (wide, narrow) in enumerate(((wide_one, narrow_one), (wide_two, narrow_two))):
        for tap in range(3):
            wide[tap] = total[:, (4 * at + tap) * COLS : (4 * at + tap + 1) * COLS]
        narrow[...] = total[:, (4 * at + 3) * COLS : (4 * at + 4) * COLS]


def body(inputs, upstream, wide_one, narrow_one, wide_two, narrow_two):
    own = pl.pallas_call(
        pack_kernel, out_shape=jax.ShapeDtypeStruct((8, 3, 8 * COLS), BF), name="pack_rows"
    )(wide_one, narrow_one, wide_two, narrow_two)
    rows_z = lax.all_to_all(own, RING_Z, 0, 0, tiled=True).reshape(24, 8 * COLS)
    x = exchange(after(inputs[0], rows_z))
    rows_one = collect_pairs(rows_z[:, : 4 * COLS], "x")
    rows_two = collect_pairs(rows_z[:, 4 * COLS :], RING_Y)
    rows_one = collect(rows_one, RING_Y)
    far_two, next_two = hop(rows_two, "x", 2), hop(rows_two, "x", 1)
    g = exchange(after(upstream[0], x))
    act1, slope_x = gelu_parts(x.astype(F32))
    act1 = act1.astype(BF)
    lower1 = jnp.concatenate([along(act1[3 * QUARTER :], 1), act1[: 3 * QUARTER]], axis=0)
    upper1 = jnp.concatenate([act1[QUARTER:], along(act1[:QUARTER], -1)], axis=0)

    channels = lax.iota(jnp.int32, ROWS)

    def unmixed(rows, x_first):
        return dot_plain((slot_owner(-1, x_first)[None, :] == channels[:, None]).astype(BF), rows).astype(BF)

    mix_one = (slot_owner(1, False)[:, None] == channels[None, :]).astype(BF)
    mix_two = (slot_owner(1, True)[:, None] == channels[None, :]).astype(BF)

    last_two = hop(rows_two, "x", 3)
    rows_one = after(rows_one, far_two, next_two, last_two, act1)
    k1 = unmixed(collect_pairs(rows_one, "core"), False)
    rows_two = collect_pairs(jnp.concatenate([rows_two, next_two, far_two, last_two], axis=0), "core")

    def tap(k, i):
        return k[:, i * COLS : (i + 1) * COLS]

    pre1 = (
        dot_plain(act1, tap(k1, 1))
        + dot_plain(lower1, tap(k1, 0))
        + dot_plain(upper1, tap(k1, 2))
    )
    inner1, slope1 = gelu_parts(pre1)
    inner1 = inner1.astype(BF)
    middle = (x.astype(F32) + dot_back(inner1, tap(k1, 3))).astype(BF)
    k2 = unmixed(after(rows_two, middle, g), True)

    half = 2 * QUARTER
    act2, slope_m = gelu_parts(middle.astype(F32))
    act2 = act2.astype(BF)
    first, third = dot_plain(act2, tap(k2, 0)), dot_plain(act2, tap(k2, 2))
    to_later = along(first[half:].astype(BF), 1).astype(F32)
    to_earlier = along(third[:half].astype(BF), -1).astype(F32)
    pre2 = (
        dot_plain(act2, tap(k2, 1))
        + jnp.concatenate([to_later, first[:half]], axis=0)
        + jnp.concatenate([third[half:], to_earlier], axis=0)
    )
    inner2, slope2 = gelu_parts(pre2)
    inner2 = inner2.astype(BF)

    dpre2 = (dot_plain(g, tap(k2, 3)) * slope2).astype(BF)
    from_later, from_earlier = along(dpre2[:half], -1), along(dpre2[half:], 1)
    trio2 = jnp.concatenate(
        [
            jnp.concatenate([dpre2[half:], from_later], axis=0),
            dpre2,
            jnp.concatenate([from_earlier, dpre2[:half]], axis=0),
        ],
        axis=1,
    )
    grads2 = jnp.concatenate([dot_rows(act2, trio2).astype(BF), dot_rows(g, inner2).astype(BF)], axis=1)
    sent2 = dot_plain(mix_two[COLS:], grads2).astype(BF)
    got2 = swap(sent2, "core", 1)
    trio2 = after(trio2, sent2)
    dact2 = dot_back(trio2, k2[:, : 3 * COLS])
    middle_grad = (g.astype(F32) + dact2 * slope_m).astype(BF)

    dpre1 = (dot_plain(middle_grad, tap(k1, 3)) * slope1).astype(BF)
    dpre1 = after(dpre1, got2)
    part2 = total_of(dot_plain(mix_two[:COLS], grads2).astype(BF), got2)
    near2, far2 = spread_half(part2, "x", 3)
    trio1 = jnp.concatenate(
        [
            jnp.concatenate([dpre1[QUARTER:], along(dpre1[:QUARTER], -1)], axis=0),
            dpre1,
            jnp.concatenate([along(dpre1[3 * QUARTER :], 1), dpre1[: 3 * QUARTER]], axis=0),
        ],
        axis=1,
    )
    dpre1 = after(dpre1, part2)
    grads1 = jnp.concatenate(
        [
            dot_rows(lower1, dpre1).astype(BF),
            dot_rows(act1, dpre1).astype(BF),
            dot_rows(upper1, dpre1).astype(BF),
            dot_rows(middle_grad, inner1).astype(BF),
        ],
        axis=1,
    )
    sent1 = dot_plain(mix_one[COLS:], grads1).astype(BF)
    got1 = swap(sent1, "core", 1)
    kept1 = dot_plain(mix_one[:COLS], after(grads1, sent1)).astype(BF)
    result = middle.astype(F32) + dot_back(after(inner2, sent1), tap(k2, 3))
    result = result.astype(BF)
    part1 = total_of(kept1, got1)
    dact1 = dot_back(after(trio1, part1), k1[:, : 3 * COLS])
    cotangent = (middle_grad.astype(F32) + dact1 * slope_x).astype(BF)
    pieces = [pair_of((after(cotangent, part1), after(result, part1)), 2)]
    part1 = spread(part1, RING_Y)
    part2 = total_of(*spread_half(total_of(near2, after(far2, part1[1])), "x", 1))
    ready = after(cotangent, part1[1]), after(result, part1[1])
    pieces += [pair_of(ready, k) for k in (1, 3)]
    cotangent = placed(cotangent, [(pair[:QUARTER], at) for pair, at in pieces])
    result = placed(result, [(pair[QUARTER:], at) for pair, at in pieces])

    part1 = spread_pairs(total_of(*part1), "x")
    part2 = spread_pairs(part2, RING_Y)
    both = jnp.concatenate([part1, part2], axis=1).reshape(8, 3, 8 * COLS)
    both = spread_pairs(both, "zq")
    wide = jax.ShapeDtypeStruct((3, 3, COLS), BF)
    narrow = jax.ShapeDtypeStruct((3, COLS), BF)
    grads = pl.pallas_call(
        unpack_kernel, out_shape=(wide, narrow, wide, narrow), name="sum_rows"
    )(both[:1], swap(both[1:], "zp", 1))
    return (result[None], cotangent[None], *grads)


def solution(mesh):
    names = ("yl", "x", "zq", "zp", "yh", "core")
    fine = Mesh(mesh.devices.reshape(2, 4, 4, 2, 2, 2), names)
    seq, batch = names[:4], names[4:]
    specs = (
        P(batch, seq, None),
        P(batch, seq, None),
        P(None, seq + batch, None),
        P(seq + batch, None),
        P(None, seq + batch, None),
        P(seq + batch, None),
    )
    return jax.shard_map(body, mesh=fine, in_specs=specs, out_specs=specs, check_vma=False)
```

```python
import jax
import jax.numpy as jnp
from jax import lax
from jax.experimental import pallas as pl
from jax.experimental.pallas import tpu as pltpu
from jax.sharding import Mesh, PartitionSpec as P

BF = jnp.bfloat16
F32 = jnp.float32
LINE = ("yl", "x")
RING_Y = ("yl", "yh")
RING_Z = ("zq", "zp")
COLS = 384
ROWS = 768
QUARTER = 128


def gelu_parts(v):
    cdf = 0.5 * (1.0 + lax.erf(v * 0.7071067811865476))
    slope = cdf + v * jnp.exp(-0.5 * v * v) * 0.3989422804014327
    return v * cdf, slope


def dot_plain(left, right):
    return jnp.dot(left, right, preferred_element_type=F32)


def dot_rows(left, right):
    return lax.dot_general(left, right, (((0,), (0,)), ((), ())), preferred_element_type=F32)


def dot_back(left, right):
    return lax.dot_general(left, right, (((1,), (1,)), ((), ())), preferred_element_type=F32)


def after(value, *others):
    return lax.optimization_barrier((value, *others))[0]


def along(array, by):
    count = lax.axis_size(LINE)
    got = lax.ppermute(array, LINE, [(i, (i + by) % count) for i in range(count)])
    end = 0 if by > 0 else count - 1
    return jnp.where(lax.axis_index(LINE) == end, jnp.zeros_like(got), got)


def permuted(array, axis, target):
    count = lax.axis_size(axis)
    place = (lambda y: y % 2 * 2 + y // 2) if axis == RING_Y else (lambda i: i)
    return lax.ppermute(array, axis, [(place(i), place(target(i) % count)) for i in range(count)])


def hop(array, axis, by):
    return permuted(array, axis, lambda i: i + by)


def swap(array, axis, bits):
    return permuted(array, axis, lambda i: i ^ bits)


def collect(rows, axis):
    count = lax.axis_size(axis)
    return jnp.concatenate([rows] + [hop(rows, axis, k) for k in range(1, count)], axis=0)


def collect_pairs(rows, axis):
    rows = jnp.concatenate([rows, swap(rows, axis, 1)], axis=0)
    if lax.axis_size(axis) == 4:
        rows = jnp.concatenate([rows, swap(rows, axis, 3)], axis=0)
    return rows


def total_of(own, *others):
    total = own.astype(F32)
    for other in others:
        total = total + other.astype(F32)
    return total.astype(BF)


def spread(rows, axis):
    count = lax.axis_size(axis)
    size = rows.shape[0] // count
    return [rows[:size]] + [hop(rows[k * size : (k + 1) * size], axis, k) for k in range(1, count)]


def spread_half(rows, axis, bits):
    half = rows.shape[0] // 2
    return rows[:half], swap(rows[half:], axis, bits)


def spread_pairs(rows, axis):
    return total_of(*spread_half(total_of(*spread_half(rows, axis, 3)), axis, 1))


def slot_owner(sign, x_first):
    slot = lax.iota(jnp.int32, ROWS)
    k = lax.div(slot, jnp.int32(3))
    row = slot - 3 * k
    kp, kq, k_in, k_out, kc = k & 1, (k >> 1) & 3, (k >> 3) & 3, (k >> 5) & 3, k >> 7
    zp, zq = kp, kq
    if sign > 0:
        zp, zq = lax.axis_index("zp") ^ kp, lax.axis_index("zq") ^ (kq ^ (kq >> 1))
    x, y = lax.axis_index("x"), lax.axis_index("yh") * 2 + lax.axis_index("yl")
    if x_first:
        y = y ^ (k_in ^ (k_in >> 1))
        x = x ^ (k_out ^ (k_out >> 1)) if sign > 0 else (x - k_out + 4) & 3
    else:
        x, y = x ^ (k_in ^ (k_in >> 1)), (y + sign * k_out + 4) & 3
    c = lax.axis_index("core") ^ kc
    yh, yl = y >> 1, y & 1
    return ((((yl * 4 + x) * 8 + zq * 2 + zp) * 2 + yh) * 2 + c) * 3 + row


def exchange(array):
    swapped = lax.all_to_all(array.reshape(4, QUARTER, ROWS), "zq", 0, 0, tiled=True)
    return swapped.reshape(4 * QUARTER, ROWS)


def pair_of(arrays, k):
    me = lax.axis_index("zq")
    at = ((me + k) & 3) * QUARTER
    sent = [lax.dynamic_slice_in_dim(array, at, QUARTER, 0) for array in arrays]
    return hop(jnp.concatenate(sent, axis=0), "zq", k), ((me + 4 - k) & 3) * QUARTER


def placed(array, pieces):
    for piece, at in pieces:
        array = lax.dynamic_update_slice_in_dim(array, piece, at, 0)
    return array


def pack_kernel(wide_one, narrow_one, wide_two, narrow_two, out):
    for at, (wide, narrow) in enumerate(((wide_one, narrow_one), (wide_two, narrow_two))):
        for copy in range(8):
            for tap in range(3):
                out[copy, :, (4 * at + tap) * COLS : (4 * at + tap + 1) * COLS] = wide[tap]
            out[copy, :, (4 * at + 3) * COLS : (4 * at + 4) * COLS] = narrow[...]


def unpack_kernel(own, got, wide_one, narrow_one, wide_two, narrow_two):
    total = (own[0].astype(F32) + got[0].astype(F32)).astype(BF)
    for at, (wide, narrow) in enumerate(((wide_one, narrow_one), (wide_two, narrow_two))):
        for tap in range(3):
            wide[tap] = total[:, (4 * at + tap) * COLS : (4 * at + tap + 1) * COLS]
        narrow[...] = total[:, (4 * at + 3) * COLS : (4 * at + 4) * COLS]


def body(inputs, upstream, wide_one, narrow_one, wide_two, narrow_two):
    own = pl.pallas_call(
        pack_kernel, out_shape=jax.ShapeDtypeStruct((8, 3, 8 * COLS), BF), name="pack_rows"
    )(wide_one, narrow_one, wide_two, narrow_two)
    rows_z = lax.all_to_all(own, RING_Z, 0, 0, tiled=True).reshape(24, 8 * COLS)
    x = exchange(after(inputs[0], rows_z))
    rows_one = collect_pairs(rows_z[:, : 4 * COLS], "x")
    rows_two = collect_pairs(rows_z[:, 4 * COLS :], RING_Y)
    rows_one = collect(rows_one, RING_Y)
    far_two, next_two = hop(rows_two, "x", 2), hop(rows_two, "x", 1)
    g = exchange(after(upstream[0], x))
    act1, slope_x = gelu_parts(x.astype(F32))
    act1 = act1.astype(BF)
    lower1 = jnp.concatenate([along(act1[3 * QUARTER :], 1), act1[: 3 * QUARTER]], axis=0)
    upper1 = jnp.concatenate([act1[QUARTER:], along(act1[:QUARTER], -1)], axis=0)

    channels = lax.iota(jnp.int32, ROWS)

    unmix_one = (slot_owner(-1, False)[None, :] == channels[:, None]).astype(BF)
    unmix_two = (slot_owner(-1, True)[None, :] == channels[:, None]).astype(BF)
    mix_one = (slot_owner(1, False)[:, None] == channels[None, :]).astype(BF)
    mix_two = (slot_owner(1, True)[:, None] == channels[None, :]).astype(BF)
    unmix_one, unmix_two = lax.optimization_barrier((unmix_one, unmix_two))
    mix_one, mix_two = lax.optimization_barrier((mix_one, mix_two))

    rows_one = after(rows_one, far_two, next_two, act1)
    k1 = dot_plain(unmix_one, collect_pairs(rows_one, "core")).astype(BF)
    last_two = hop(after(rows_two, k1), "x", 3)
    rows_two = jnp.concatenate([rows_two, next_two, far_two, last_two], axis=0)

    def tap(k, i):
        return k[:, i * COLS : (i + 1) * COLS]

    pre1 = (
        dot_plain(act1, tap(k1, 1))
        + dot_plain(lower1, tap(k1, 0))
        + dot_plain(upper1, tap(k1, 2))
    )
    inner1, slope1 = gelu_parts(pre1)
    inner1 = inner1.astype(BF)
    middle = (x.astype(F32) + dot_back(inner1, tap(k1, 3))).astype(BF)
    rows_two = collect_pairs(after(rows_two, middle), "core")
    k2 = dot_plain(unmix_two, rows_two).astype(BF)

    half = 2 * QUARTER
    act2, slope_m = gelu_parts(middle.astype(F32))
    act2 = act2.astype(BF)
    first, third = dot_plain(act2, tap(k2, 0)), dot_plain(act2, tap(k2, 2))
    to_later = along(first[half:].astype(BF), 1).astype(F32)
    to_earlier = along(third[:half].astype(BF), -1).astype(F32)
    pre2 = (
        dot_plain(act2, tap(k2, 1))
        + jnp.concatenate([to_later, first[:half]], axis=0)
        + jnp.concatenate([third[half:], to_earlier], axis=0)
    )
    inner2, slope2 = gelu_parts(pre2)
    inner2 = inner2.astype(BF)

    dpre2 = (dot_plain(g, tap(k2, 3)) * slope2).astype(BF)
    from_later, from_earlier = along(dpre2[:half], -1), along(dpre2[half:], 1)
    trio2 = jnp.concatenate(
        [
            jnp.concatenate([dpre2[half:], from_later], axis=0),
            dpre2,
            jnp.concatenate([from_earlier, dpre2[:half]], axis=0),
        ],
        axis=1,
    )
    grads2 = jnp.concatenate([dot_rows(act2, trio2).astype(BF), dot_rows(g, inner2).astype(BF)], axis=1)
    sent2 = dot_plain(mix_two[COLS:], grads2).astype(BF)
    got2 = swap(sent2, "core", 1)
    trio2 = after(trio2, sent2)
    dact2 = dot_back(trio2, k2[:, : 3 * COLS])
    middle_grad = (g.astype(F32) + dact2 * slope_m).astype(BF)

    dpre1 = (dot_plain(middle_grad, tap(k1, 3)) * slope1).astype(BF)
    dpre1 = after(dpre1, got2)
    part2 = total_of(dot_plain(mix_two[:COLS], grads2).astype(BF), got2)
    near2, far2 = spread_half(part2, "x", 3)
    trio1 = jnp.concatenate(
        [
            jnp.concatenate([dpre1[QUARTER:], along(dpre1[:QUARTER], -1)], axis=0),
            dpre1,
            jnp.concatenate([along(dpre1[3 * QUARTER :], 1), dpre1[: 3 * QUARTER]], axis=0),
        ],
        axis=1,
    )
    dpre1 = after(dpre1, part2)
    grads1 = jnp.concatenate(
        [
            dot_rows(lower1, dpre1).astype(BF),
            dot_rows(act1, dpre1).astype(BF),
            dot_rows(upper1, dpre1).astype(BF),
            dot_rows(middle_grad, inner1).astype(BF),
        ],
        axis=1,
    )
    sent1 = dot_plain(mix_one[COLS:], grads1).astype(BF)
    got1 = swap(sent1, "core", 1)
    kept1 = dot_plain(mix_one[:COLS], after(grads1, sent1)).astype(BF)
    result = middle.astype(F32) + dot_back(after(inner2, sent1), tap(k2, 3))
    result = result.astype(BF)
    part1 = total_of(kept1, got1)
    dact1 = dot_back(after(trio1, part1), k1[:, : 3 * COLS])
    cotangent = (middle_grad.astype(F32) + dact1 * slope_x).astype(BF)
    pieces = [pair_of((after(cotangent, part1), after(result, part1)), 2)]
    part1 = spread(part1, RING_Y)
    part2 = total_of(*spread_half(total_of(near2, after(far2, part1[1])), "x", 1))
    ready = after(cotangent, part1[1]), after(result, part1[1])
    pieces += [pair_of(ready, k) for k in (1, 3)]
    cotangent = placed(cotangent, [(pair[:QUARTER], at) for pair, at in pieces])
    result = placed(result, [(pair[QUARTER:], at) for pair, at in pieces])

    part1 = spread_pairs(total_of(*part1), "x")
    part2 = spread_pairs(part2, RING_Y)
    both = jnp.concatenate([part1, part2], axis=1).reshape(8, 3, 8 * COLS)
    both = spread_pairs(both, "zq")
    wide = jax.ShapeDtypeStruct((3, 3, COLS), BF)
    narrow = jax.ShapeDtypeStruct((3, COLS), BF)
    grads = pl.pallas_call(
        unpack_kernel, out_shape=(wide, narrow, wide, narrow), name="sum_rows"
    )(both[:1], swap(both[1:], "zp", 1))
    return (result[None], cotangent[None], *grads)


def solution(mesh):
    names = ("yl", "x", "zq", "zp", "yh", "core")
    fine = Mesh(mesh.devices.reshape(2, 4, 4, 2, 2, 2), names)
    seq, batch = names[:4], names[4:]
    specs = (
        P(batch, seq, None),
        P(batch, seq, None),
        P(None, seq + batch, None),
        P(seq + batch, None),
        P(None, seq + batch, None),
        P(seq + batch, None),
    )
    return jax.shard_map(body, mesh=fine, in_specs=specs, out_specs=specs, check_vma=False)
```

```python
import jax
import jax.numpy as jnp
from jax import lax
from jax.experimental import pallas as pl
from jax.experimental.pallas import tpu as pltpu
from jax.sharding import Mesh, PartitionSpec as P

BF = jnp.bfloat16
F32 = jnp.float32
LINE = ("yl", "x")
RING_Y = ("yl", "yh")
RING_Z = ("zq", "zp")
COLS = 384
ROWS = 768
QUARTER = 128


def gelu_parts(v):
    cdf = 0.5 * (1.0 + lax.erf(v * 0.7071067811865476))
    slope = cdf + v * jnp.exp(-0.5 * v * v) * 0.3989422804014327
    return v * cdf, slope


def dot_plain(left, right):
    return jnp.dot(left, right, preferred_element_type=F32)


def dot_rows(left, right):
    return lax.dot_general(left, right, (((0,), (0,)), ((), ())), preferred_element_type=F32)


def dot_back(left, right):
    return lax.dot_general(left, right, (((1,), (1,)), ((), ())), preferred_element_type=F32)


def after(value, *others):
    return lax.optimization_barrier((value, *others))[0]


def along(array, by):
    count = lax.axis_size(LINE)
    got = lax.ppermute(array, LINE, [(i, (i + by) % count) for i in range(count)])
    end = 0 if by > 0 else count - 1
    return jnp.where(lax.axis_index(LINE) == end, jnp.zeros_like(got), got)


def permuted(array, axis, target):
    count = lax.axis_size(axis)
    place = (lambda y: y % 2 * 2 + y // 2) if axis == RING_Y else (lambda i: i)
    return lax.ppermute(array, axis, [(place(i), place(target(i) % count)) for i in range(count)])


def hop(array, axis, by):
    return permuted(array, axis, lambda i: i + by)


def swap(array, axis, bits):
    return permuted(array, axis, lambda i: i ^ bits)


def collect(rows, axis):
    count = lax.axis_size(axis)
    return jnp.concatenate([rows] + [hop(rows, axis, k) for k in range(1, count)], axis=0)


def collect_pairs(rows, axis):
    rows = jnp.concatenate([rows, swap(rows, axis, 1)], axis=0)
    if lax.axis_size(axis) == 4:
        rows = jnp.concatenate([rows, swap(rows, axis, 3)], axis=0)
    return rows


def total_of(own, *others):
    total = own.astype(F32)
    for other in others:
        total = total + other.astype(F32)
    return total.astype(BF)


def spread(rows, axis):
    count = lax.axis_size(axis)
    size = rows.shape[0] // count
    return [rows[:size]] + [hop(rows[k * size : (k + 1) * size], axis, k) for k in range(1, count)]


def spread_half(rows, axis, bits):
    half = rows.shape[0] // 2
    return rows[:half], swap(rows[half:], axis, bits)


def spread_pairs(rows, axis):
    return total_of(*spread_half(total_of(*spread_half(rows, axis, 3)), axis, 1))


def slot_owner(sign, x_first):
    slot = lax.iota(jnp.int32, ROWS)
    k = lax.div(slot, jnp.int32(3))
    row = slot - 3 * k
    kp, kq, k_in, k_out, kc = k & 1, (k >> 1) & 3, (k >> 3) & 3, (k >> 5) & 3, k >> 7
    zp, zq = kp, kq
    if sign > 0:
        zp, zq = lax.axis_index("zp") ^ kp, lax.axis_index("zq") ^ (kq ^ (kq >> 1))
    x, y = lax.axis_index("x"), lax.axis_index("yh") * 2 + lax.axis_index("yl")
    if x_first:
        y = y ^ (k_in ^ (k_in >> 1))
        x = x ^ (k_out ^ (k_out >> 1)) if sign > 0 else (x - k_out + 4) & 3
    else:
        x, y = x ^ (k_in ^ (k_in >> 1)), (y + sign * k_out + 4) & 3
    c = lax.axis_index("core") ^ kc
    yh, yl = y >> 1, y & 1
    return ((((yl * 4 + x) * 8 + zq * 2 + zp) * 2 + yh) * 2 + c) * 3 + row


def exchange(*arrays):
    blocks = [array.reshape(4, QUARTER, ROWS) for array in arrays]
    swapped = lax.all_to_all(jnp.concatenate(blocks, axis=1), "zq", 0, 0, tiled=True)
    return [
        swapped[:, i * QUARTER : (i + 1) * QUARTER].reshape(4 * QUARTER, ROWS)
        for i in range(len(arrays))
    ]


def pair_of(arrays, k):
    me = lax.axis_index("zq")
    at = ((me + k) & 3) * QUARTER
    sent = [lax.dynamic_slice_in_dim(array, at, QUARTER, 0) for array in arrays]
    return hop(jnp.concatenate(sent, axis=0), "zq", k), ((me + 4 - k) & 3) * QUARTER


def placed(array, pieces):
    for piece, at in pieces:
        array = lax.dynamic_update_slice_in_dim(array, piece, at, 0)
    return array


def pack_kernel(wide_one, narrow_one, wide_two, narrow_two, out):
    for at, (wide, narrow) in enumerate(((wide_one, narrow_one), (wide_two, narrow_two))):
        for copy in range(8):
            for tap in range(3):
                out[copy, :, (4 * at + tap) * COLS : (4 * at + tap + 1) * COLS] = wide[tap]
            out[copy, :, (4 * at + 3) * COLS : (4 * at + 4) * COLS] = narrow[...]


def unpack_kernel(own, got, wide_one, narrow_one, wide_two, narrow_two):
    total = (own[0].astype(F32) + got[0].astype(F32)).astype(BF)
    for at, (wide, narrow) in enumerate(((wide_one, narrow_one), (wide_two, narrow_two))):
        for tap in range(3):
            wide[tap] = total[:, (4 * at + tap) * COLS : (4 * at + tap + 1) * COLS]
        narrow[...] = total[:, (4 * at + 3) * COLS : (4 * at + 4) * COLS]


def body(inputs, upstream, wide_one, narrow_one, wide_two, narrow_two):
    own = pl.pallas_call(
        pack_kernel, out_shape=jax.ShapeDtypeStruct((8, 3, 8 * COLS), BF), name="pack_rows"
    )(wide_one, narrow_one, wide_two, narrow_two)
    rows_z = lax.all_to_all(own, RING_Z, 0, 0, tiled=True).reshape(24, 8 * COLS)
    x, g = exchange(after(inputs[0], rows_z), upstream[0])
    rows_one = collect_pairs(rows_z[:, : 4 * COLS], "x")
    rows_two = collect_pairs(rows_z[:, 4 * COLS :], RING_Y)
    rows_one = collect(rows_one, RING_Y)
    far_two, next_two = hop(rows_two, "x", 2), hop(rows_two, "x", 1)
    act1, slope_x = gelu_parts(x.astype(F32))
    act1 = act1.astype(BF)
    lower1 = jnp.concatenate([along(act1[3 * QUARTER :], 1), act1[: 3 * QUARTER]], axis=0)
    upper1 = jnp.concatenate([act1[QUARTER:], along(act1[:QUARTER], -1)], axis=0)

    channels = lax.iota(jnp.int32, ROWS)

    unmix_one = (slot_owner(-1, False)[None, :] == channels[:, None]).astype(BF)
    unmix_two = (slot_owner(-1, True)[None, :] == channels[:, None]).astype(BF)
    mix_one = (slot_owner(1, False)[:, None] == channels[None, :]).astype(BF)
    mix_two = (slot_owner(1, True)[:, None] == channels[None, :]).astype(BF)
    unmix_one, unmix_two = lax.optimization_barrier((unmix_one, unmix_two))
    mix_one, mix_two = lax.optimization_barrier((mix_one, mix_two))

    rows_one = after(rows_one, far_two, next_two)
    k1 = dot_plain(unmix_one, collect_pairs(rows_one, "core")).astype(BF)
    last_two = hop(rows_two, "x", 3)
    rows_two = jnp.concatenate([rows_two, next_two, far_two, last_two], axis=0)

    def tap(k, i):
        return k[:, i * COLS : (i + 1) * COLS]

    pre1 = (
        dot_plain(act1, tap(k1, 1))
        + dot_plain(lower1, tap(k1, 0))
        + dot_plain(upper1, tap(k1, 2))
    )
    inner1, slope1 = gelu_parts(pre1)
    inner1 = inner1.astype(BF)
    middle = (x.astype(F32) + dot_back(inner1, tap(k1, 3))).astype(BF)
    rows_two = collect_pairs(after(rows_two, middle), "core")
    k2 = dot_plain(unmix_two, rows_two).astype(BF)

    half = 2 * QUARTER
    act2, slope_m = gelu_parts(middle.astype(F32))
    act2 = act2.astype(BF)
    first, third = dot_plain(act2, tap(k2, 0)), dot_plain(act2, tap(k2, 2))
    to_later = along(first[half:].astype(BF), 1).astype(F32)
    to_earlier = along(third[:half].astype(BF), -1).astype(F32)
    pre2 = (
        dot_plain(act2, tap(k2, 1))
        + jnp.concatenate([to_later, first[:half]], axis=0)
        + jnp.concatenate([third[half:], to_earlier], axis=0)
    )
    inner2, slope2 = gelu_parts(pre2)
    inner2 = inner2.astype(BF)

    dpre2 = (dot_plain(g, tap(k2, 3)) * slope2).astype(BF)
    from_later, from_earlier = along(dpre2[:half], -1), along(dpre2[half:], 1)
    trio2 = jnp.concatenate(
        [
            jnp.concatenate([dpre2[half:], from_later], axis=0),
            dpre2,
            jnp.concatenate([from_earlier, dpre2[:half]], axis=0),
        ],
        axis=1,
    )
    grads2 = jnp.concatenate([dot_rows(act2, trio2).astype(BF), dot_rows(g, inner2).astype(BF)], axis=1)
    sent2 = dot_plain(mix_two[COLS:], grads2).astype(BF)
    got2 = swap(sent2, "core", 1)
    trio2 = after(trio2, sent2)
    dact2 = dot_back(trio2, k2[:, : 3 * COLS])
    middle_grad = (g.astype(F32) + dact2 * slope_m).astype(BF)

    dpre1 = (dot_plain(middle_grad, tap(k1, 3)) * slope1).astype(BF)
    dpre1 = after(dpre1, got2)
    part2 = total_of(dot_plain(mix_two[:COLS], grads2).astype(BF), got2)
    near2, far2 = spread_half(part2, "x", 3)
    trio1 = jnp.concatenate(
        [
            jnp.concatenate([dpre1[QUARTER:], along(dpre1[:QUARTER], -1)], axis=0),
            dpre1,
            jnp.concatenate([along(dpre1[3 * QUARTER :], 1), dpre1[: 3 * QUARTER]], axis=0),
        ],
        axis=1,
    )
    dpre1 = after(dpre1, part2)
    grads1 = jnp.concatenate(
        [
            dot_rows(lower1, dpre1).astype(BF),
            dot_rows(act1, dpre1).astype(BF),
            dot_rows(upper1, dpre1).astype(BF),
            dot_rows(middle_grad, inner1).astype(BF),
        ],
        axis=1,
    )
    sent1 = dot_plain(mix_one[COLS:], grads1).astype(BF)
    got1 = swap(sent1, "core", 1)
    kept1 = dot_plain(mix_one[:COLS], after(grads1, sent1)).astype(BF)
    result = middle.astype(F32) + dot_back(after(inner2, sent1), tap(k2, 3))
    result = result.astype(BF)
    part1 = total_of(kept1, got1)
    dact1 = dot_back(after(trio1, part1), k1[:, : 3 * COLS])
    cotangent = (middle_grad.astype(F32) + dact1 * slope_x).astype(BF)
    pieces = [pair_of((after(cotangent, part1), after(result, part1)), 2)]
    part1 = spread(part1, RING_Y)
    part2 = total_of(*spread_half(total_of(near2, after(far2, part1[1])), "x", 1))
    ready = after(cotangent, part1[1]), after(result, part1[1])
    pieces += [pair_of(ready, k) for k in (1, 3)]
    cotangent = placed(cotangent, [(pair[:QUARTER], at) for pair, at in pieces])
    result = placed(result, [(pair[QUARTER:], at) for pair, at in pieces])

    part1 = spread_pairs(total_of(*part1), "x")
    part2 = spread_pairs(part2, RING_Y)
    both = jnp.concatenate([part1, part2], axis=1).reshape(8, 3, 8 * COLS)
    both = spread_pairs(both, "zq")
    wide = jax.ShapeDtypeStruct((3, 3, COLS), BF)
    narrow = jax.ShapeDtypeStruct((3, COLS), BF)
    grads = pl.pallas_call(
        unpack_kernel, out_shape=(wide, narrow, wide, narrow), name="sum_rows"
    )(both[:1], swap(both[1:], "zp", 1))
    return (result[None], cotangent[None], *grads)


def solution(mesh):
    names = ("yl", "x", "zq", "zp", "yh", "core")
    fine = Mesh(mesh.devices.reshape(2, 4, 4, 2, 2, 2), names)
    seq, batch = names[:4], names[4:]
    specs = (
        P(batch, seq, None),
        P(batch, seq, None),
        P(None, seq + batch, None),
        P(seq + batch, None),
        P(None, seq + batch, None),
        P(seq + batch, None),
    )
    return jax.shard_map(body, mesh=fine, in_specs=specs, out_specs=specs, check_vma=False)
```

```python
import jax
import jax.numpy as jnp
from jax import lax
from jax.experimental import pallas as pl
from jax.experimental.pallas import tpu as pltpu
from jax.sharding import Mesh, PartitionSpec as P

BF = jnp.bfloat16
F32 = jnp.float32
LINE = ("yl", "x")
RING_Y = ("yl", "yh")
RING_Z = ("zq", "zp")
COLS = 384
ROWS = 768
QUARTER = 128


def gelu_parts(v):
    cdf = 0.5 * (1.0 + lax.erf(v * 0.7071067811865476))
    slope = cdf + v * jnp.exp(-0.5 * v * v) * 0.3989422804014327
    return v * cdf, slope


def dot_plain(left, right):
    return jnp.dot(left, right, preferred_element_type=F32)


def dot_rows(left, right):
    return lax.dot_general(left, right, (((0,), (0,)), ((), ())), preferred_element_type=F32)


def dot_back(left, right):
    return lax.dot_general(left, right, (((1,), (1,)), ((), ())), preferred_element_type=F32)


def after(value, *others):
    return lax.optimization_barrier((value, *others))[0]


def along(array, by):
    count = lax.axis_size(LINE)
    got = lax.ppermute(array, LINE, [(i, (i + by) % count) for i in range(count)])
    end = 0 if by > 0 else count - 1
    return jnp.where(lax.axis_index(LINE) == end, jnp.zeros_like(got), got)


def permuted(array, axis, target):
    count = lax.axis_size(axis)
    place = (lambda y: y % 2 * 2 + y // 2) if axis == RING_Y else (lambda i: i)
    return lax.ppermute(array, axis, [(place(i), place(target(i) % count)) for i in range(count)])


def hop(array, axis, by):
    return permuted(array, axis, lambda i: i + by)


def swap(array, axis, bits):
    return permuted(array, axis, lambda i: i ^ bits)


def collect(rows, axis):
    count = lax.axis_size(axis)
    return jnp.concatenate([rows] + [hop(rows, axis, k) for k in range(1, count)], axis=0)


def collect_pairs(rows, axis):
    rows = jnp.concatenate([rows, swap(rows, axis, 1)], axis=0)
    if lax.axis_size(axis) == 4:
        rows = jnp.concatenate([rows, swap(rows, axis, 3)], axis=0)
    return rows


def total_of(own, *others):
    total = own.astype(F32)
    for other in others:
        total = total + other.astype(F32)
    return total.astype(BF)


def spread(rows, axis):
    count = lax.axis_size(axis)
    size = rows.shape[0] // count
    return [rows[:size]] + [hop(rows[k * size : (k + 1) * size], axis, k) for k in range(1, count)]


def spread_half(rows, axis, bits):
    half = rows.shape[0] // 2
    return rows[:half], swap(rows[half:], axis, bits)


def spread_pairs(rows, axis):
    return total_of(*spread_half(total_of(*spread_half(rows, axis, 3)), axis, 1))


def slot_owner(sign, x_first):
    slot = lax.iota(jnp.int32, ROWS)
    k = lax.div(slot, jnp.int32(3))
    row = slot - 3 * k
    kp, kq, k_in, k_out, kc = k & 1, (k >> 1) & 3, (k >> 3) & 3, (k >> 5) & 3, k >> 7
    zp, zq = kp, kq
    if sign > 0:
        zp, zq = lax.axis_index("zp") ^ kp, lax.axis_index("zq") ^ (kq ^ (kq >> 1))
    x, y = lax.axis_index("x"), lax.axis_index("yh") * 2 + lax.axis_index("yl")
    if x_first:
        y = y ^ (k_in ^ (k_in >> 1))
        x = x ^ (k_out ^ (k_out >> 1)) if sign > 0 else (x - k_out + 4) & 3
    else:
        x, y = x ^ (k_in ^ (k_in >> 1)), (y + sign * k_out + 4) & 3
    c = lax.axis_index("core") ^ kc
    yh, yl = y >> 1, y & 1
    return ((((yl * 4 + x) * 8 + zq * 2 + zp) * 2 + yh) * 2 + c) * 3 + row


def exchange(*arrays):
    blocks = [array.reshape(4, QUARTER, ROWS) for array in arrays]
    swapped = lax.all_to_all(jnp.concatenate(blocks, axis=1), "zq", 0, 0, tiled=True)
    return [
        swapped[:, i * QUARTER : (i + 1) * QUARTER].reshape(4 * QUARTER, ROWS)
        for i in range(len(arrays))
    ]


def pair_of(arrays, k):
    me = lax.axis_index("zq")
    at = ((me + k) & 3) * QUARTER
    sent = [lax.dynamic_slice_in_dim(array, at, QUARTER, 0) for array in arrays]
    return hop(jnp.concatenate(sent, axis=0), "zq", k), ((me + 4 - k) & 3) * QUARTER


def placed(array, pieces):
    for piece, at in pieces:
        array = lax.dynamic_update_slice_in_dim(array, piece, at, 0)
    return array


def unmix_kernel(order, own, got, out):
    half = order.shape[1] // 2
    total = jnp.dot(order[:, :half], own[...], preferred_element_type=F32)
    total = total + jnp.dot(order[:, half:], got[...], preferred_element_type=F32)
    out[...] = total.astype(BF)


def unmixed(order, own, got):
    rows, cols = own.shape
    half = pl.BlockSpec((rows, COLS), lambda i: (0, i))
    return pl.pallas_call(
        unmix_kernel,
        grid=(cols // COLS,),
        in_specs=[pl.BlockSpec((ROWS, ROWS), lambda i: (0, 0)), half, half],
        out_specs=pl.BlockSpec((ROWS, COLS), lambda i: (0, i)),
        out_shape=jax.ShapeDtypeStruct((ROWS, cols), BF),
        compiler_params=pltpu.CompilerParams(vmem_limit_bytes=32 * 1024 * 1024),
        cost_estimate=pl.CostEstimate(
            flops=2 * ROWS * ROWS * cols, bytes_accessed=2 * ROWS * (ROWS + 2 * cols), transcendentals=0
        ),
        name="unmix_rows",
    )(order, own, got)


def pack_kernel(wide_one, narrow_one, wide_two, narrow_two, out):
    for at, (wide, narrow) in enumerate(((wide_one, narrow_one), (wide_two, narrow_two))):
        for copy in range(8):
            for tap in range(3):
                out[copy, :, (4 * at + tap) * COLS : (4 * at + tap + 1) * COLS] = wide[tap]
            out[copy, :, (4 * at + 3) * COLS : (4 * at + 4) * COLS] = narrow[...]


def unpack_kernel(own, got, wide_one, narrow_one, wide_two, narrow_two):
    total = (own[0].astype(F32) + got[0].astype(F32)).astype(BF)
    for at, (wide, narrow) in enumerate(((wide_one, narrow_one), (wide_two, narrow_two))):
        for tap in range(3):
            wide[tap] = total[:, (4 * at + tap) * COLS : (4 * at + tap + 1) * COLS]
        narrow[...] = total[:, (4 * at + 3) * COLS : (4 * at + 4) * COLS]


def body(inputs, upstream, wide_one, narrow_one, wide_two, narrow_two):
    own = pl.pallas_call(
        pack_kernel, out_shape=jax.ShapeDtypeStruct((8, 3, 8 * COLS), BF), name="pack_rows"
    )(wide_one, narrow_one, wide_two, narrow_two)
    rows_z = lax.all_to_all(own, RING_Z, 0, 0, tiled=True).reshape(24, 8 * COLS)
    x, g = exchange(after(inputs[0], rows_z), upstream[0])
    rows_one = collect_pairs(rows_z[:, : 4 * COLS], "x")
    rows_two = collect_pairs(rows_z[:, 4 * COLS :], RING_Y)
    rows_one = collect(rows_one, RING_Y)
    far_two, next_two = hop(rows_two, "x", 2), hop(rows_two, "x", 1)
    act1, slope_x = gelu_parts(x.astype(F32))
    act1 = act1.astype(BF)
    lower1 = jnp.concatenate([along(act1[3 * QUARTER :], 1), act1[: 3 * QUARTER]], axis=0)
    upper1 = jnp.concatenate([act1[QUARTER:], along(act1[:QUARTER], -1)], axis=0)

    channels = lax.iota(jnp.int32, ROWS)

    unmix_one = (slot_owner(-1, False)[None, :] == channels[:, None]).astype(BF)
    unmix_two = (slot_owner(-1, True)[None, :] == channels[:, None]).astype(BF)
    mix_one = (slot_owner(1, False)[:, None] == channels[None, :]).astype(BF)
    mix_two = (slot_owner(1, True)[:, None] == channels[None, :]).astype(BF)
    unmix_one, unmix_two = lax.optimization_barrier((unmix_one, unmix_two))
    mix_one, mix_two = lax.optimization_barrier((mix_one, mix_two))

    rows_one = after(rows_one, far_two, next_two)
    k1 = unmixed(unmix_one, after(rows_one, act1), swap(rows_one, "core", 1))
    last_two = hop(rows_two, "x", 3)
    rows_two = jnp.concatenate([rows_two, next_two, far_two, last_two], axis=0)

    def tap(k, i):
        return k[:, i * COLS : (i + 1) * COLS]

    pre1 = (
        dot_plain(act1, tap(k1, 1))
        + dot_plain(lower1, tap(k1, 0))
        + dot_plain(upper1, tap(k1, 2))
    )
    inner1, slope1 = gelu_parts(pre1)
    inner1 = inner1.astype(BF)
    middle = (x.astype(F32) + dot_back(inner1, tap(k1, 3))).astype(BF)
    rows_two = after(rows_two, k1)
    k2 = unmixed(unmix_two, rows_two, swap(rows_two, "core", 1))

    half = 2 * QUARTER
    act2, slope_m = gelu_parts(middle.astype(F32))
    act2 = act2.astype(BF)
    first, third = dot_plain(act2, tap(k2, 0)), dot_plain(act2, tap(k2, 2))
    to_later = along(first[half:].astype(BF), 1).astype(F32)
    to_earlier = along(third[:half].astype(BF), -1).astype(F32)
    pre2 = (
        dot_plain(act2, tap(k2, 1))
        + jnp.concatenate([to_later, first[:half]], axis=0)
        + jnp.concatenate([third[half:], to_earlier], axis=0)
    )
    inner2, slope2 = gelu_parts(pre2)
    inner2 = inner2.astype(BF)

    dpre2 = (dot_plain(g, tap(k2, 3)) * slope2).astype(BF)
    from_later, from_earlier = along(dpre2[:half], -1), along(dpre2[half:], 1)
    trio2 = jnp.concatenate(
        [
            jnp.concatenate([dpre2[half:], from_later], axis=0),
            dpre2,
            jnp.concatenate([from_earlier, dpre2[:half]], axis=0),
        ],
        axis=1,
    )
    grads2 = jnp.concatenate([dot_rows(act2, trio2).astype(BF), dot_rows(g, inner2).astype(BF)], axis=1)
    sent2 = dot_plain(mix_two[COLS:], grads2).astype(BF)
    got2 = swap(sent2, "core", 1)
    trio2 = after(trio2, sent2)
    dact2 = dot_back(trio2, k2[:, : 3 * COLS])
    middle_grad = (g.astype(F32) + dact2 * slope_m).astype(BF)

    dpre1 = (dot_plain(middle_grad, tap(k1, 3)) * slope1).astype(BF)
    dpre1 = after(dpre1, got2)
    part2 = total_of(dot_plain(mix_two[:COLS], grads2).astype(BF), got2)
    near2, far2 = spread_half(part2, "x", 3)
    trio1 = jnp.concatenate(
        [
            jnp.concatenate([dpre1[QUARTER:], along(dpre1[:QUARTER], -1)], axis=0),
            dpre1,
            jnp.concatenate([along(dpre1[3 * QUARTER :], 1), dpre1[: 3 * QUARTER]], axis=0),
        ],
        axis=1,
    )
    dpre1 = after(dpre1, part2)
    grads1 = jnp.concatenate(
        [
            dot_rows(lower1, dpre1).astype(BF),
            dot_rows(act1, dpre1).astype(BF),
            dot_rows(upper1, dpre1).astype(BF),
            dot_rows(middle_grad, inner1).astype(BF),
        ],
        axis=1,
    )
    sent1 = dot_plain(mix_one[COLS:], grads1).astype(BF)
    got1 = swap(sent1, "core", 1)
    kept1 = dot_plain(mix_one[:COLS], after(grads1, sent1)).astype(BF)
    result = middle.astype(F32) + dot_back(after(inner2, sent1), tap(k2, 3))
    result = result.astype(BF)
    part1 = total_of(kept1, got1)
    dact1 = dot_back(after(trio1, part1), k1[:, : 3 * COLS])
    cotangent = (middle_grad.astype(F32) + dact1 * slope_x).astype(BF)
    pieces = [pair_of((after(cotangent, part1), after(result, part1)), 2)]
    part1 = spread(part1, RING_Y)
    part2 = total_of(*spread_half(total_of(near2, after(far2, part1[1])), "x", 1))
    ready = after(cotangent, part1[1]), after(result, part1[1])
    pieces += [pair_of(ready, k) for k in (1, 3)]
    cotangent = placed(cotangent, [(pair[:QUARTER], at) for pair, at in pieces])
    result = placed(result, [(pair[QUARTER:], at) for pair, at in pieces])

    part1 = spread_pairs(total_of(*part1), "x")
    part2 = spread_pairs(part2, RING_Y)
    both = jnp.concatenate([part1, part2], axis=1).reshape(8, 3, 8 * COLS)
    both = spread_pairs(both, "zq")
    wide = jax.ShapeDtypeStruct((3, 3, COLS), BF)
    narrow = jax.ShapeDtypeStruct((3, COLS), BF)
    grads = pl.pallas_call(
        unpack_kernel, out_shape=(wide, narrow, wide, narrow), name="sum_rows"
    )(both[:1], swap(both[1:], "zp", 1))
    return (result[None], cotangent[None], *grads)


def solution(mesh):
    names = ("yl", "x", "zq", "zp", "yh", "core")
    fine = Mesh(mesh.devices.reshape(2, 4, 4, 2, 2, 2), names)
    seq, batch = names[:4], names[4:]
    specs = (
        P(batch, seq, None),
        P(batch, seq, None),
        P(None, seq + batch, None),
        P(seq + batch, None),
        P(None, seq + batch, None),
        P(seq + batch, None),
    )
    return jax.shard_map(body, mesh=fine, in_specs=specs, out_specs=specs, check_vma=False)
```

```python
import jax
import jax.numpy as jnp
from jax import lax
from jax.experimental import pallas as pl
from jax.experimental.pallas import tpu as pltpu
from jax.sharding import Mesh, PartitionSpec as P

BF = jnp.bfloat16
F32 = jnp.float32
LINE = ("yl", "x")
RING_Y = ("yl", "yh")
RING_Z = ("zq", "zp")
COLS = 384
ROWS = 768
QUARTER = 128


def gelu_parts(v):
    cdf = 0.5 * (1.0 + lax.erf(v * 0.7071067811865476))
    slope = cdf + v * jnp.exp(-0.5 * v * v) * 0.3989422804014327
    return v * cdf, slope


def dot_plain(left, right):
    return jnp.dot(left, right, preferred_element_type=F32)


def dot_rows(left, right):
    return lax.dot_general(left, right, (((0,), (0,)), ((), ())), preferred_element_type=F32)


def dot_back(left, right):
    return lax.dot_general(left, right, (((1,), (1,)), ((), ())), preferred_element_type=F32)


def after(value, *others):
    return lax.optimization_barrier((value, *others))[0]


def along(array, by):
    count = lax.axis_size(LINE)
    got = lax.ppermute(array, LINE, [(i, (i + by) % count) for i in range(count)])
    end = 0 if by > 0 else count - 1
    return jnp.where(lax.axis_index(LINE) == end, jnp.zeros_like(got), got)


def permuted(array, axis, target):
    count = lax.axis_size(axis)
    place = (lambda y: y % 2 * 2 + y // 2) if axis == RING_Y else (lambda i: i)
    return lax.ppermute(array, axis, [(place(i), place(target(i) % count)) for i in range(count)])


def hop(array, axis, by):
    return permuted(array, axis, lambda i: i + by)


def swap(array, axis, bits):
    return permuted(array, axis, lambda i: i ^ bits)


def collect(rows, axis):
    count = lax.axis_size(axis)
    return jnp.concatenate([rows] + [hop(rows, axis, k) for k in range(1, count)], axis=0)


def collect_pairs(rows, axis):
    rows = jnp.concatenate([rows, swap(rows, axis, 1)], axis=0)
    if lax.axis_size(axis) == 4:
        rows = jnp.concatenate([rows, swap(rows, axis, 3)], axis=0)
    return rows


def total_of(own, *others):
    total = own.astype(F32)
    for other in others:
        total = total + other.astype(F32)
    return total.astype(BF)


def spread(rows, axis):
    count = lax.axis_size(axis)
    size = rows.shape[0] // count
    return [rows[:size]] + [hop(rows[k * size : (k + 1) * size], axis, k) for k in range(1, count)]


def spread_half(rows, axis, bits):
    half = rows.shape[0] // 2
    return rows[:half], swap(rows[half:], axis, bits)


def spread_pairs(rows, axis):
    return total_of(*spread_half(total_of(*spread_half(rows, axis, 3)), axis, 1))


def slot_owner(sign, x_first):
    slot = lax.iota(jnp.int32, ROWS)
    k = lax.div(slot, jnp.int32(3))
    row = slot - 3 * k
    kp, kq, k_in, k_out, kc = k & 1, (k >> 1) & 3, (k >> 3) & 3, (k >> 5) & 3, k >> 7
    zp, zq = kp, kq
    if sign > 0:
        zp, zq = lax.axis_index("zp") ^ kp, lax.axis_index("zq") ^ (kq ^ (kq >> 1))
    x, y = lax.axis_index("x"), lax.axis_index("yh") * 2 + lax.axis_index("yl")
    if x_first:
        y = y ^ (k_in ^ (k_in >> 1))
        x = x ^ (k_out ^ (k_out >> 1)) if sign > 0 else (x - k_out + 4) & 3
    else:
        x, y = x ^ (k_in ^ (k_in >> 1)), (y + sign * k_out + 4) & 3
    c = lax.axis_index("core") ^ kc
    yh, yl = y >> 1, y & 1
    return ((((yl * 4 + x) * 8 + zq * 2 + zp) * 2 + yh) * 2 + c) * 3 + row


def exchange(*arrays):
    blocks = [array.reshape(4, QUARTER, ROWS) for array in arrays]
    swapped = lax.all_to_all(jnp.concatenate(blocks, axis=1), "zq", 0, 0, tiled=True)
    return [
        swapped[:, i * QUARTER : (i + 1) * QUARTER].reshape(4 * QUARTER, ROWS)
        for i in range(len(arrays))
    ]


def pair_of(arrays, k):
    me = lax.axis_index("zq")
    at = ((me + k) & 3) * QUARTER
    sent = [lax.dynamic_slice_in_dim(array, at, QUARTER, 0) for array in arrays]
    return hop(jnp.concatenate(sent, axis=0), "zq", k), ((me + 4 - k) & 3) * QUARTER


def placed(array, pieces):
    for piece, at in pieces:
        array = lax.dynamic_update_slice_in_dim(array, piece, at, 0)
    return array


def unmix_kernel(order, own, got, out):
    half = order.shape[1] // 2
    total = jnp.dot(order[:, :half], own[...], preferred_element_type=F32)
    total = total + jnp.dot(order[:, half:], got[...], preferred_element_type=F32)
    out[...] = total.astype(BF)


def unmixed(order, own, got):
    rows, cols = own.shape
    half = pl.BlockSpec((rows, COLS), lambda i: (0, i))
    return pl.pallas_call(
        unmix_kernel,
        grid=(cols // COLS,),
        in_specs=[pl.BlockSpec((ROWS, ROWS), lambda i: (0, 0)), half, half],
        out_specs=pl.BlockSpec((ROWS, COLS), lambda i: (0, i)),
        out_shape=jax.ShapeDtypeStruct((ROWS, cols), BF),
        compiler_params=pltpu.CompilerParams(vmem_limit_bytes=32 * 1024 * 1024),
        cost_estimate=pl.CostEstimate(
            flops=2 * ROWS * ROWS * cols, bytes_accessed=2 * ROWS * (ROWS + 2 * cols), transcendentals=0
        ),
        name="unmix_rows",
    )(order, own, got)


def pack_kernel(wide_one, narrow_one, wide_two, narrow_two, out):
    for at, (wide, narrow) in enumerate(((wide_one, narrow_one), (wide_two, narrow_two))):
        for copy in range(8):
            for tap in range(3):
                out[copy, :, (4 * at + tap) * COLS : (4 * at + tap + 1) * COLS] = wide[tap]
            out[copy, :, (4 * at + 3) * COLS : (4 * at + 4) * COLS] = narrow[...]


def unpack_kernel(own, got, wide_one, narrow_one, wide_two, narrow_two):
    total = (own[0].astype(F32) + got[0].astype(F32)).astype(BF)
    for at, (wide, narrow) in enumerate(((wide_one, narrow_one), (wide_two, narrow_two))):
        for tap in range(3):
            wide[tap] = total[:, (4 * at + tap) * COLS : (4 * at + tap + 1) * COLS]
        narrow[...] = total[:, (4 * at + 3) * COLS : (4 * at + 4) * COLS]


def body(inputs, upstream, wide_one, narrow_one, wide_two, narrow_two):
    own = pl.pallas_call(
        pack_kernel, out_shape=jax.ShapeDtypeStruct((8, 3, 8 * COLS), BF), name="pack_rows"
    )(wide_one, narrow_one, wide_two, narrow_two)
    rows_z = lax.all_to_all(own, RING_Z, 0, 0, tiled=True).reshape(24, 8 * COLS)
    x, g = exchange(after(inputs[0], rows_z), upstream[0])
    rows_one = collect_pairs(rows_z[:, : 4 * COLS], "x")
    rows_two = collect_pairs(rows_z[:, 4 * COLS :], RING_Y)
    rows_one = collect(rows_one, RING_Y)
    far_two, next_two = hop(rows_two, "x", 2), hop(rows_two, "x", 1)
    act1, slope_x = gelu_parts(x.astype(F32))
    act1 = act1.astype(BF)
    lower1 = jnp.concatenate([along(act1[3 * QUARTER :], 1), act1[: 3 * QUARTER]], axis=0)
    upper1 = jnp.concatenate([act1[QUARTER:], along(act1[:QUARTER], -1)], axis=0)

    channels = lax.iota(jnp.int32, ROWS)

    unmix_one = (slot_owner(-1, False)[None, :] == channels[:, None]).astype(BF)
    unmix_two = (slot_owner(-1, True)[None, :] == channels[:, None]).astype(BF)
    mix_one = (slot_owner(1, False)[:, None] == channels[None, :]).astype(BF)
    mix_two = (slot_owner(1, True)[:, None] == channels[None, :]).astype(BF)
    unmix_one, unmix_two = lax.optimization_barrier((unmix_one, unmix_two))
    mix_one, mix_two = lax.optimization_barrier((mix_one, mix_two))

    rows_one = after(rows_one, far_two, next_two)
    k1 = unmixed(unmix_one, after(rows_one, act1), swap(rows_one, "core", 1))
    last_two = hop(rows_two, "x", 3)
    rows_two = jnp.concatenate([rows_two, next_two, far_two, last_two], axis=0)

    def tap(k, i):
        return k[:, i * COLS : (i + 1) * COLS]

    pre1 = (
        dot_plain(act1, tap(k1, 1))
        + dot_plain(lower1, tap(k1, 0))
        + dot_plain(upper1, tap(k1, 2))
    )
    inner1, slope1 = gelu_parts(pre1)
    inner1 = inner1.astype(BF)
    middle = (x.astype(F32) + dot_back(inner1, tap(k1, 3))).astype(BF)
    rows_two = after(rows_two, k1)
    k2 = unmixed(unmix_two, rows_two, swap(rows_two, "core", 1))

    half = 2 * QUARTER
    act2, slope_m = gelu_parts(middle.astype(F32))
    act2 = act2.astype(BF)
    first, third = dot_plain(act2, tap(k2, 0)), dot_plain(act2, tap(k2, 2))
    to_later = along(first[half:].astype(BF), 1).astype(F32)
    to_earlier = along(third[:half].astype(BF), -1).astype(F32)
    pre2 = (
        dot_plain(act2, tap(k2, 1))
        + jnp.concatenate([to_later, first[:half]], axis=0)
        + jnp.concatenate([third[half:], to_earlier], axis=0)
    )
    inner2, slope2 = gelu_parts(pre2)
    inner2 = inner2.astype(BF)

    dpre2 = (dot_plain(g, tap(k2, 3)) * slope2).astype(BF)
    from_later, from_earlier = along(dpre2[:half], -1), along(dpre2[half:], 1)
    trio2 = jnp.concatenate(
        [
            jnp.concatenate([dpre2[half:], from_later], axis=0),
            dpre2,
            jnp.concatenate([from_earlier, dpre2[:half]], axis=0),
        ],
        axis=1,
    )
    grads2 = jnp.concatenate([dot_rows(act2, trio2).astype(BF), dot_rows(g, inner2).astype(BF)], axis=1)
    sent2 = dot_plain(mix_two[COLS:], grads2).astype(BF)
    got2 = swap(sent2, "core", 1)
    trio2 = after(trio2, sent2)
    dact2 = dot_back(trio2, k2[:, : 3 * COLS])
    middle_grad = (g.astype(F32) + dact2 * slope_m).astype(BF)

    dpre1 = (dot_plain(middle_grad, tap(k1, 3)) * slope1).astype(BF)
    dpre1 = after(dpre1, got2)
    part2 = total_of(dot_plain(mix_two[:COLS], grads2).astype(BF), got2)
    near2, far2 = spread_half(part2, "x", 3)
    trio1 = jnp.concatenate(
        [
            jnp.concatenate([dpre1[QUARTER:], along(dpre1[:QUARTER], -1)], axis=0),
            dpre1,
            jnp.concatenate([along(dpre1[3 * QUARTER :], 1), dpre1[: 3 * QUARTER]], axis=0),
        ],
        axis=1,
    )
    dpre1 = after(dpre1, part2)
    grads1 = jnp.concatenate(
        [
            dot_rows(lower1, dpre1).astype(BF),
            dot_rows(act1, dpre1).astype(BF),
            dot_rows(upper1, dpre1).astype(BF),
            dot_rows(middle_grad, inner1).astype(BF),
        ],
        axis=1,
    )
    sent1 = dot_plain(mix_one[COLS:], grads1).astype(BF)
    got1 = swap(sent1, "core", 1)
    kept1 = dot_plain(mix_one[:COLS], after(grads1, sent1)).astype(BF)
    result = middle.astype(F32) + dot_back(after(inner2, sent1), tap(k2, 3))
    result = result.astype(BF)
    part1 = total_of(kept1, got1)
    dact1 = dot_back(after(trio1, part1), k1[:, : 3 * COLS])
    cotangent = (middle_grad.astype(F32) + dact1 * slope_x).astype(BF)
    part1 = spread(part1, RING_Y)
    part2 = total_of(*spread_half(total_of(near2, after(far2, part1[1])), "x", 1))
    ready = after(cotangent, part1[1]), after(result, part1[1])
    pieces = [pair_of(ready, k) for k in (2, 1, 3)]
    cotangent = placed(cotangent, [(pair[:QUARTER], at) for pair, at in pieces])
    result = placed(result, [(pair[QUARTER:], at) for pair, at in pieces])

    part1 = spread_pairs(total_of(*part1), "x")
    part2 = spread_pairs(part2, RING_Y)
    both = jnp.concatenate([part1, part2], axis=1).reshape(8, 3, 8 * COLS)
    both = spread_pairs(both, "zq")
    wide = jax.ShapeDtypeStruct((3, 3, COLS), BF)
    narrow = jax.ShapeDtypeStruct((3, COLS), BF)
    grads = pl.pallas_call(
        unpack_kernel, out_shape=(wide, narrow, wide, narrow), name="sum_rows"
    )(both[:1], swap(both[1:], "zp", 1))
    return (result[None], cotangent[None], *grads)


def solution(mesh):
    names = ("yl", "x", "zq", "zp", "yh", "core")
    fine = Mesh(mesh.devices.reshape(2, 4, 4, 2, 2, 2), names)
    seq, batch = names[:4], names[4:]
    specs = (
        P(batch, seq, None),
        P(batch, seq, None),
        P(None, seq + batch, None),
        P(seq + batch, None),
        P(None, seq + batch, None),
        P(seq + batch, None),
    )
    return jax.shard_map(body, mesh=fine, in_specs=specs, out_specs=specs, check_vma=False)
```
